256 devices in a mesh: samp: 16 (over x, y_hi, core), var: 8 (over z), row: 2 (over y_lo).
Axes of the slice: x: 4, y: 4 (y_hi: 2, y_lo: 2; y = y_hi * 2 + y_lo), z: 8, core: 2. Of those that a mesh axis runs over, the one named last changes fastest.
Arguments:
- col_dosage: bfloat16 [2, 2048, 8192], P(None, 'var', 'samp'), may hold values from 0 to 1
- col_ancestry: bfloat16 [3, 2, 2048, 8192], P(None, None, 'var', 'samp'), may hold values from 0 to 1, as said below
- row_dosage: bfloat16 [2, 2048, 4096], P(None, 'var', ('row', 'samp')), may hold values from 0 to 1
- row_ancestry: bfloat16 [3, 2, 2048, 4096], P(None, None, 'var', ('row', 'samp')), may hold values from 0 to 1, as said below
Outputs:
- kinship: float32 [4096, 3, 8192], P(('row', 'var'), None, 'samp')
The draws below stay inside these ranges and needn't reach their ends.
Inputs may be any that keep to these rules, and one draw needn't show every extreme that they name: `col_ancestry`: posteriors are positive and the three of a haplotype sum to at most about one (after rounding to bfloat16); the remainder is the chance that the call is missing. `row_ancestry`: as for col_ancestry.
All inputs are finite; a program needn't handle non-finite values.
Results may differ from the reference program's by a relative error of at most 0.00063.
Values may be sent and summed in bfloat16 or wider, within the bound.
A program may use at most 64 MiB of HBM per device.

```python
import jax
import jax.numpy as jnp

VARS = 2048
ROWS = 4096
COLS = 8192
N_VAR = 8


def ramp_values(count, low, high):
    return low + (high - low) * jnp.arange(count, dtype=jnp.float32) / count


def dosage_levels(base, level_key, count):
    level = jax.random.uniform(level_key, (VARS,), jnp.float32, 0.4, 1.0) * ramp_values(VARS, 0.5, 1.0)
    across = ramp_values(count, 0.3, 0.9)
    return (base * level[None, :, None] * across[None, None, :]).astype(jnp.bfloat16)


def posterior_shares(raw, missing, count):
    tilt = ramp_values(count, -1.0, 1.0)
    raw = raw.at[0].add(tilt[None, None, :])
    weights = jnp.exp(raw)
    return (weights / (jnp.sum(weights, axis=0, keepdims=True) + missing[None])).astype(jnp.bfloat16)


def draw_col_dosage(key, part):
    key = jax.random.fold_in(key, 11)
    first, second = jax.random.split(key)
    base = jax.random.uniform(first, (2, VARS, COLS), jnp.float32)
    return dosage_levels(base, second, COLS)


def draw_row_dosage(key, part):
    key = jax.random.fold_in(key, 12)
    first, second = jax.random.split(key)
    base = jax.random.uniform(first, (2, VARS, ROWS), jnp.float32)
    return dosage_levels(base, second, ROWS)


def draw_col_ancestry(key, part):
    key = jax.random.fold_in(key, 13)
    first, second = jax.random.split(key)
    raw = 1.5 * jax.random.normal(first, (3, 2, VARS, COLS), jnp.float32)
    missing = 0.3 * jnp.exp(jax.random.normal(second, (2, VARS, COLS), jnp.float32))
    return posterior_shares(raw, missing, COLS)


def draw_row_ancestry(key, part):
    key = jax.random.fold_in(key, 14)
    first, second = jax.random.split(key)
    raw = 1.5 * jax.random.normal(first, (3, 2, VARS, ROWS), jnp.float32)
    missing = 0.3 * jnp.exp(jax.random.normal(second, (2, VARS, ROWS), jnp.float32))
    return posterior_shares(raw, missing, ROWS)


def setup_inputs(seed: int = 0) -> dict:
    arg_keys = jax.random.split(jax.random.key(seed), 5)
    return {
        "col_dosage": draw_col_dosage(jax.random.fold_in(arg_keys[4], 71), 0),
        "col_ancestry": draw_col_ancestry(jax.random.fold_in(arg_keys[4], 71), 0),
        "row_dosage": draw_row_dosage(jax.random.fold_in(arg_keys[4], 71), 0),
        "row_ancestry": draw_row_ancestry(jax.random.fold_in(arg_keys[4], 71), 0),
    }


def centre(dosage, ancestry, freq):
    values = dosage.astype(jnp.float32)
    shares = ancestry.astype(jnp.float32)
    return jnp.sum(shares * (values[None] - freq[:, None, :, None]), axis=1).astype(jnp.bfloat16)


def reference(col_dosage, col_ancestry, row_dosage, row_ancestry):
    values = col_dosage.astype(jnp.float32)
    shares = col_ancestry.astype(jnp.float32)
    counts = jnp.sum(shares, axis=(1, 3))
    sums = jnp.sum(shares * values[None], axis=(1, 3))
    freq = sums / counts
    spread = jnp.sum(freq * (1.0 - freq), axis=1)
    col_centred = centre(col_dosage, col_ancestry, freq)
    row_centred = centre(row_dosage, row_ancestry, freq)
    width = VARS // N_VAR
    total = jnp.zeros((ROWS, 3, COLS), jnp.float32)
    for group in range(N_VAR):
        rows_part = row_centred[:, group * width:(group + 1) * width].astype(jnp.float32)
        cols_part = col_centred[:, group * width:(group + 1) * width].astype(jnp.float32)
        total = total + jnp.einsum('avr,avc->rac', rows_part, cols_part)
    return total / spread[None, :, None]
```

```python
import functools

import jax
import jax.numpy as jnp
from jax import lax
from jax.experimental import pallas as pl
from jax.experimental.pallas import tpu as pltpu
from jax.sharding import PartitionSpec as P

MESH = pl.DeviceIdType.MESH
F32 = jnp.float32
BF16 = jnp.bfloat16
HALVES = 2


def device(s, z, r):
    return {"samp": s, "var": z, "row": r}


def aligned(value, size):
    return pl.multiple_of(value, size)


def kernel(
    sizes,
    cd_hbm,
    ca_hbm,
    rd_hbm,
    ra_hbm,
    out_hbm,
    spread_ref,
    cd,
    ca,
    rd,
    ra,
    pst,
    stat,
    freq,
    spreads,
    rows_t,
    a_buf,
    b_buf,
    c_send,
    c_recv,
    o_buf,
    in_sem,
    out_sem,
    stat_send,
    stat_recv,
    spread_send,
    spread_recv,
    t_send,
    t_recv,
    g_send,
    g_recv,
    f_send,
    f_recv,
    b_send,
    b_recv,
    c_ssem,
    c_rsem,
):
    ns, nz, nr = sizes
    np_ = ns // 2
    s, z, r = lax.axis_index("samp"), lax.axis_index("var"), lax.axis_index("row")
    p, c = s // 2, s % 2
    sib = s + 1 - 2 * c
    other = 1 - r
    na = ca.shape[0]
    nv = cd.shape[1]
    kv = nv // nr
    cols = cd.shape[2]
    wide = cols // HALVES
    chunks = na * HALVES
    piece = 128 // np_

    loads = [
        pltpu.make_async_copy(src, dst, in_sem.at[i])
        for i, (src, dst) in enumerate(((cd_hbm, cd), (ca_hbm, ca), (rd_hbm, rd), (ra_hbm, ra)))
    ]
    for load in loads:
        load.start()

    barrier = pltpu.get_barrier_semaphore()

    def greet(who):
        pl.semaphore_signal(barrier, inc=1, device_id=who, device_id_type=MESH)

    for i in range(1, ns):
        greet(device((s + i) % ns, z, r))
    for i in range(1, nz):
        greet(device(s, (z + i) % nz, r))
    greet(device(s, z, other))
    for k in range(nz):
        for ry in range(nr):
            own = (p == z) & (k == z) & (ry == r)

            @pl.when(jnp.logical_not(own))
            def _():
                greet(device(z * 2 + c, k, ry))

    loads[0].wait()
    loads[1].wait()
    step = 32

    def fold(x):
        total = x[:, :128]
        for t in range(1, cols // 128):
            total = total + x[:, t * 128:(t + 1) * 128]
        return total

    def stats(i, carry):
        rows = pl.ds(aligned(i * step, step), step)
        dosage = [cd[h, rows, :].astype(F32) for h in range(2)]
        for a in range(na):
            share = [ca[a, h, rows, :].astype(F32) for h in range(2)]
            pst[a, rows, :] = fold(share[0] + share[1])
            pst[4 + a, rows, :] = fold(share[0] * dosage[0] + share[1] * dosage[1])
        return carry

    lax.fori_loop(0, nv // step, stats, 0)
    for a in range(na):
        for k in (a, 4 + a):
            stat[s, k:k + 1, :] = jnp.sum(pst[k].T, axis=0, keepdims=True)
    for k in (3, 7):
        stat[s, k:k + 1, :] = jnp.ones((1, nv), F32)

    pl.semaphore_wait(barrier, (ns - 1) + (nz - 1) + 1 + nz * nr - jnp.where(p == z, 1, 0))

    sent = []

    def push(src, dst, send_sem, recv_sem, who):
        copy = pltpu.make_async_remote_copy(
            src_ref=src, dst_ref=dst, send_sem=send_sem, recv_sem=recv_sem, device_id=who, device_id_type=MESH
        )
        copy.start()
        sent.append(copy)

    def arrive(dst, sem):
        pltpu.make_async_copy(dst, dst, sem).wait()

    for i in range(1, ns):
        push(stat.at[s], stat.at[s], stat_send.at[i], stat_recv.at[i], device((s + i) % ns, z, r))
    for i in range(1, ns):
        arrive(stat.at[(s + ns - i) % ns], stat_recv.at[i])
    total = stat[0]
    for i in range(1, ns):
        total = total + stat[i]
    ratio = total[4:8] / total[0:4]
    spreads[z, 0:4, :] = jnp.broadcast_to(jnp.sum(ratio * (1.0 - ratio), axis=1, keepdims=True), (4, 128))
    spreads[z, 4:8, :] = jnp.zeros((4, 128), F32)
    for a in range(na):
        freq[a] = jnp.broadcast_to(ratio[a:a + 1, :], (128, nv)).T

    loads[2].wait()
    loads[3].wait()
    for a in range(na):
        centred = ra[a, 0].astype(F32) * (rd[0].astype(F32) - freq[a])
        centred = centred + ra[a, 1].astype(F32) * (rd[1].astype(F32) - freq[a])
        turned = centred.T.astype(BF16)
        for k in range(nr):
            rows_t[a, k] = turned[:, k * kv:(k + 1) * kv]

    def block(ry, core, e, zz):
        return a_buf.at[:, ry, pl.ds(aligned(core * 128 + e * piece, piece), piece), pl.ds(aligned(zz * kv, kv), kv)]

    for e in range(np_):
        for k in range(nr):
            src = rows_t.at[:, k, pl.ds(e * piece, piece), :]
            own = (p == e) & (p == z) & (k == r)
            number = e * nr + k

            @pl.when(own)
            def _():
                pltpu.make_async_copy(src, block(r, c, p, z), t_recv.at[z * nr + r]).start()

            @pl.when(jnp.logical_not(own))
            def _():
                pltpu.make_async_remote_copy(
                    src_ref=src,
                    dst_ref=block(r, c, e, z),
                    send_sem=t_send.at[number],
                    recv_sem=t_recv.at[z * nr + r],
                    device_id=device(e * 2 + c, p, k),
                    device_id_type=MESH,
                ).start()

    def centre(a):
        def part(i, carry):
            at = pl.ds(aligned(r * kv + i * step, step), step)
            to = pl.ds(aligned(z * kv + i * step, step), step)
            f = freq[a, at, :]
            f = jnp.concatenate([f] * (wide // 128), axis=1)
            for half in range(HALVES):
                lanes = pl.ds(half * wide, wide)
                value = ca[a, 0, at, lanes].astype(F32) * (cd[0, at, lanes].astype(F32) - f)
                value = value + ca[a, 1, at, lanes].astype(F32) * (cd[1, at, lanes].astype(F32) - f)
                b_buf[a * HALVES + half, to, :] = value.astype(BF16)
            return carry

        lax.fori_loop(0, kv // step, part, 0)

    def b_rows(j, zz, first=0, count=None):
        count = kv if count is None else count
        return b_buf.at[j, pl.ds(aligned(zz * kv + first, 64), count), :]

    far = nz // 2
    ways = (1, nz - 1)

    def b_part(j, zz, way, d):
        if d == far:
            return b_rows(j, zz, way * (kv // 2), kv // 2)
        return b_rows(j, zz)

    def b_move(j, way, d):
        origin = (z + (nz - ways[way]) * (d - 1)) % nz
        ref = b_part(j, origin, way, d)
        push(ref, ref, b_send.at[j, way, d - 1], b_recv.at[j, way, d - 1], device(s, (z + ways[way]) % nz, r))

    def b_arrive(j, way, d):
        origin = (z + (nz - ways[way]) * d) % nz
        arrive(b_part(j, origin, way, d), b_recv.at[j, way, d - 1])

    def a_piece(a, core, e):
        return a_buf.at[a, :, pl.ds(aligned(core * 128 + e * piece, piece), piece), :]

    def a_spread(a):
        for i in range(1, np_):
            q = (p + i) % np_
            push(a_piece(a, c, p), a_piece(a, c, p), g_send.at[a, i], g_recv.at[a, i], device(q * 2 + c, z, r))
        push(a_piece(a, c, p), a_piece(a, c, p), f_send.at[a, 0], f_recv.at[a, 0], device(sib, z, r))

    def a_collect(a):
        for i in range(1, np_):
            q = (p + np_ - i) % np_
            arrive(a_piece(a, c, q), g_recv.at[a, i])
            push(a_piece(a, c, q), a_piece(a, c, q), f_send.at[a, i], f_recv.at[a, i], device(sib, z, r))
        for i in range(np_):
            q = (p + np_ - i) % np_
            arrive(a_piece(a, 1 - c, q), f_recv.at[a, i])

    def multiply(j):
        a, half = j // HALVES, j % HALVES
        b = b_buf[j]
        c_send[j] = jnp.dot(a_buf[a, other], b, preferred_element_type=F32)
        push(c_send.at[j], c_recv.at[j], c_ssem.at[j], c_rsem.at[j], device(s, z, other))
        o_buf[a, :, pl.ds(half * wide, wide)] = jnp.dot(a_buf[a, r], b, preferred_element_type=F32)

    stores = []

    def finish(j):
        a, half = j // HALVES, j % HALVES
        arrive(c_recv.at[j], c_rsem.at[j])
        o_buf[a, :, pl.ds(half * wide, wide)] += c_recv[j]
        if half == HALVES - 1:
            store = pltpu.make_async_copy(o_buf.at[a], out_hbm.at[a], out_sem.at[a])
            store.start()
            stores.append(store)

    def launch(pair):
        for j in pair:
            for way in range(2):
                b_move(j, way, 1)

    pairs = [tuple(range(a * HALVES, (a + 1) * HALVES)) for a in range(na)]
    lead = far - 1
    for tick in range(lead * (na - 1) + far + 1):
        for a, pair in enumerate(pairs):
            d = tick - lead * a
            if d == 0:
                if tick == 0:
                    centre(a)
                launch(pair)
            elif 1 <= d <= far:
                for j in pair:
                    for way in range(2):
                        b_arrive(j, way, d)
                        if d < far:
                            b_move(j, way, d + 1)
                if d == far:
                    for j in pair:
                        multiply(j)
                    if a > 0:
                        for j in pairs[a - 1]:
                            finish(j)
        if tick == 0:
            for i in range(1, nz):
                push(
                    spreads.at[z], spreads.at[z], spread_send.at[i], spread_recv.at[i], device(s, (z + i) % nz, r)
                )
            for zz in range(nz):
                for ry in range(nr):
                    arrive(block(ry, c, p, zz), t_recv.at[zz * nr + ry])
            for a in range(na):
                a_spread(a)
            for a in range(1, na):
                centre(a)
        if tick >= 1 and tick % 2 == 1 and tick // 2 < na:
            a_collect(tick // 2)
    for i in range(1, nz):
        arrive(spreads.at[(z + nz - i) % nz], spread_recv.at[i])
    spread = spreads[0]
    for i in range(1, nz):
        spread = spread + spreads[i]
    spread_ref[...] = spread
    for j in pairs[-1]:
        finish(j)

    for e in range(np_):
        for k in range(nr):
            own = (p == e) & (p == z) & (k == r)
            src = rows_t.at[:, k, pl.ds(e * piece, piece), :]

            @pl.when(jnp.logical_not(own))
            def _():
                pltpu.make_async_copy(src, src, t_send.at[e * nr + k]).wait()

    for copy in sent:
        copy.wait_send()
    for store in stores:
        store.wait()


def local(sizes, col_dosage, col_ancestry, row_dosage, row_ancestry):
    ns, nz, nr = sizes
    np_ = ns // 2
    na = col_ancestry.shape[0]
    nv, cols = col_dosage.shape[1:]
    rows = row_dosage.shape[2]
    kv = nv // nr
    tall = 2 * rows
    wide = cols // HALVES
    chunks = na * HALVES
    far = nz // 2
    dma = pltpu.SemaphoreType.DMA
    total, spread = pl.pallas_call(
        functools.partial(kernel, sizes),
        out_shape=(
            jax.ShapeDtypeStruct((na, tall, cols), F32),
            jax.ShapeDtypeStruct((8, 128), F32),
        ),
        in_specs=[pl.BlockSpec(memory_space=pl.ANY)] * 4,
        out_specs=(pl.BlockSpec(memory_space=pl.ANY), pl.BlockSpec(memory_space=pltpu.VMEM)),
        scratch_shapes=[
            pltpu.VMEM(col_dosage.shape, BF16),
            pltpu.VMEM(col_ancestry.shape, BF16),
            pltpu.VMEM(row_dosage.shape, BF16),
            pltpu.VMEM(row_ancestry.shape, BF16),
            pltpu.VMEM((8, nv, 128), F32),
            pltpu.VMEM((ns, 8, nv), F32),
            pltpu.VMEM((na, nv, 128), F32),
            pltpu.VMEM((nz, 8, 128), F32),
            pltpu.VMEM((na, nr, rows, kv), BF16),
            pltpu.VMEM((na, nr, tall, nz * kv), BF16),
            pltpu.VMEM((chunks, nz * kv, wide), BF16),
            pltpu.VMEM((chunks, tall, wide), F32),
            pltpu.VMEM((chunks, tall, wide), F32),
            pltpu.VMEM((na, tall, cols), F32),
            dma((4,)),
            dma((na,)),
            dma((ns,)),
            dma((ns,)),
            dma((nz,)),
            dma((nz,)),
            dma((np_ * nr,)),
            dma((nz * nr,)),
            dma((na, np_)),
            dma((na, np_)),
            dma((na, np_)),
            dma((na, np_)),
            dma((chunks, 2, far)),
            dma((chunks, 2, far)),
            dma((chunks,)),
            dma((chunks,)),
        ],
        compiler_params=pltpu.CompilerParams(
            collective_id=0, has_side_effects=True, vmem_limit_bytes=48 * 1024 * 1024
        ),
    )(col_dosage, col_ancestry, row_dosage, row_ancestry)
    return jnp.transpose(total / spread[:na, :1][:, :, None], (1, 0, 2))


def solution(mesh):
    sizes = (mesh.shape["samp"], mesh.shape["var"], mesh.shape["row"])
    placed = (
        P(None, "var", "samp"),
        P(None, None, "var", "samp"),
        P(None, "var", ("row", "samp")),
        P(None, None, "var", ("row", "samp")),
    )
    return jax.shard_map(
        functools.partial(local, sizes),
        mesh=mesh,
        in_specs=placed,
        out_specs=P(("row", "var"), None, "samp"),
        check_vma=False,
    )
```

```python
import functools

import jax
import jax.numpy as jnp
from jax import lax
from jax.experimental import pallas as pl
from jax.experimental.pallas import tpu as pltpu
from jax.sharding import PartitionSpec as P

MESH = pl.DeviceIdType.MESH
F32 = jnp.float32
BF16 = jnp.bfloat16
HALVES = 2
STEP = 32


def device(s, z, r):
    return {"samp": s, "var": z, "row": r}


def aligned(value, size):
    return pl.multiple_of(value, size)


def kernel(
    sizes,
    cd_hbm,
    ca_hbm,
    rd_hbm,
    ra_hbm,
    out_ref,
    spread_ref,
    cd,
    ca,
    rd,
    ra,
    pst,
    part,
    stat,
    ratios,
    freq,
    spreads,
    turned,
    raw,
    centred,
    hold,
    a_buf,
    a_far,
    b_buf,
    c_send,
    c_recv,
    o_buf,
    in_sem,
    out_sem,
    pair_sem,
    stat_sem,
    spread_sem,
    t1_sem,
    t2_sem,
    g1_sem,
    g2_sem,
    f_sem,
    far_sem,
    b_sem,
    c_sem,
):
    ns, nz, nr = sizes
    nx, np_ = ns // 4, ns // 2
    s, z, r = lax.axis_index("samp"), lax.axis_index("var"), lax.axis_index("row")
    x, h, c = s // 4, (s // 2) % 2, s % 2
    p = s // 2
    other = 1 - r
    na = ca.shape[0]
    nv, cols = cd.shape[1:]
    kv = nv // nr
    wide = cols // HALVES
    piece = rd.shape[2] // np_
    far = nz // 2
    sibling = device(s + 1 - 2 * c, z, r)
    mate = device(s, z, other)
    across = device((x * 2 + 1 - h) * 2 + c, z, other)

    def chip(q):
        return q * 2 + c

    loads = [
        pltpu.make_async_copy(src, dst, in_sem.at[i])
        for i, (src, dst) in enumerate(((cd_hbm, cd), (ca_hbm, ca), (rd_hbm, rd), (ra_hbm, ra)))
    ]
    for load in loads:
        load.start()

    barrier = pltpu.get_barrier_semaphore()

    def greet(who):
        pl.semaphore_signal(barrier, inc=1, device_id=who, device_id_type=MESH)

    greet(sibling)
    for i in range(1, nz):
        greet(device(s, (z + i) % nz, r))
    for i in range(np_):
        for k in range(nr):
            if i or k:
                greet(device(chip((p + i) % np_), z, (r + k) % nr))

    loads[0].wait()
    loads[1].wait()

    def fold(value):
        total = value[:, :128]
        for t in range(1, cols // 128):
            total = total + value[:, t * 128:(t + 1) * 128]
        return total

    def stats(i, carry):
        rows = pl.ds(aligned(i * STEP, STEP), STEP)
        dosage = [cd[k, rows, :].astype(F32) for k in range(2)]
        for a in range(na):
            share = [ca[a, k, rows, :].astype(F32) for k in range(2)]
            pst[a, rows, :] = fold(share[0] + share[1])
            pst[4 + a, rows, :] = fold(share[0] * dosage[0] + share[1] * dosage[1])
        return carry

    lax.fori_loop(0, nv // STEP, stats, 0)
    for a in range(na):
        for k in (a, 4 + a):
            part[c, k:k + 1, :] = jnp.sum(pst[k].T, axis=0, keepdims=True)
    for k in (3, 7):
        part[c, k:k + 1, :] = jnp.ones((1, nv), F32)

    pl.semaphore_wait(barrier, 1 + (nz - 1) + np_ * nr - 1)

    sent = []

    def push(src, dst, sems, who):
        copy = pltpu.make_async_remote_copy(
            src_ref=src, dst_ref=dst, send_sem=sems[0], recv_sem=sems[1], device_id=who, device_id_type=MESH
        )
        copy.start()
        sent.append(copy)

    def pair(ref, *at):
        return ref.at[(0, *at)], ref.at[(1, *at)]

    def arrive(dst, sems):
        pltpu.make_async_copy(dst, dst, sems[1]).wait()

    push(part.at[c], part.at[c], pair(pair_sem, 0), sibling)

    loads[2].wait()
    loads[3].wait()
    for k in range(2):
        turned[k] = rd[k].astype(F32).T.astype(BF16)
        for a in range(na):
            turned[2 + 2 * a + k] = ra[a, k].astype(F32).T.astype(BF16)

    arrive(part.at[1 - c], pair(pair_sem, 0))
    stat[p] = part[0] + part[1]
    for i in range(1, nx):
        push(stat.at[p], stat.at[p], pair(stat_sem, 0, i), device(chip(((x + i) % nx) * 2 + h), z, r))
    for i in range(nx):
        push(stat.at[p], stat.at[p], pair(stat_sem, 1, i), device(chip(((x + i) % nx) * 2 + 1 - h), z, other))

    def t1_piece(i, k):
        rows = pl.ds(aligned(((p + i) % np_) * piece, piece), piece)
        half = pl.ds(aligned((1 - (r + k) % nr) * kv, kv), kv)
        return turned.at[:, rows, half], raw.at[:, p, r]

    own = pltpu.make_async_copy(*t1_piece(0, 0), t1_sem.at[1, 0, 0])
    own.start()
    for i in range(np_):
        for k in range(nr):
            if i or k:
                push(*t1_piece(i, k), pair(t1_sem, i, k), device(chip((p + i) % np_), z, (r + k) % nr))

    for i in range(1, nx):
        arrive(stat.at[((x + nx - i) % nx) * 2 + h], pair(stat_sem, 0, i))
    for i in range(nx):
        arrive(stat.at[((x + nx - i) % nx) * 2 + 1 - h], pair(stat_sem, 1, i))
    total = stat[0]
    for i in range(1, np_):
        total = total + stat[i]
    ratio = total[4:8] / total[0:4]
    ratios[0:4, :] = ratio
    for a in range(na):
        freq[a] = jnp.broadcast_to(ratio[a:a + 1, :], (128, nv)).T

    for i in range(np_):
        for k in range(nr):
            arrive(raw.at[:, (p + np_ - i) % np_, (r + nr - k) % nr], pair(t1_sem, i, k))

    def centre_rows(a):
        f = ratios[a:a + 1, pl.ds(aligned(other * kv, kv), kv)]
        f = jnp.broadcast_to(f, (piece, kv))[None, None]
        value = raw[2 + 2 * a].astype(F32) * (raw[0].astype(F32) - f)
        value = value + raw[3 + 2 * a].astype(F32) * (raw[1].astype(F32) - f)
        centred[a] = value.astype(BF16)
        hold[a, :, :, pl.ds(aligned(z * kv, kv), kv)] = centred[a, z]

    def hold_from(a, zz):
        return hold.at[a, :, :, pl.ds(aligned(zz * kv, kv), kv)]

    def t2_send(a):
        for i in range(1, nz):
            to = (z + i) % nz
            push(centred.at[a, to], hold_from(a, z), pair(t2_sem, a, i), device(s, to, r))

    def a_rows(a, ry, core, first, count):
        return a_buf.at[a, ry, pl.ds(aligned(core * 128 + first * piece, piece), count * piece), :]

    def t2_wait(a):
        for i in range(1, nz):
            arrive(hold_from(a, (z + nz - i) % nz), pair(t2_sem, a, i))

    def g1_send(a, o):
        ry = r if o == 0 else other
        for k, who in enumerate((mate, across)):
            push(hold.at[a, ry], a_rows(a, ry, c, p, 1), pair(g1_sem, a, o, k), who)

    def g1_wait(a, o):
        ry = other if o == 0 else r
        arrive(a_rows(a, ry, c, p, 1), pair(g1_sem, a, o, 0))
        arrive(a_rows(a, ry, c, x * 2 + 1 - h, 1), pair(g1_sem, a, o, 1))

    def g2_send(a, o):
        ry = other if o == 0 else r
        ref = a_rows(a, ry, c, x * 2, 2)
        for i in range(1, nx):
            push(ref, ref, pair(g2_sem, a, o, i), device(chip(((x + i) % nx) * 2 + h), z, r))
        push(ref, ref, pair(f_sem, a, o, 0), sibling)

    def g2_wait(a, o):
        ry = other if o == 0 else r
        for i in range(1, nx):
            ref = a_rows(a, ry, c, ((x + nx - i) % nx) * 2, 2)
            arrive(ref, pair(g2_sem, a, o, i))
            push(ref, ref, pair(f_sem, a, o, i), sibling)

    def f_wait(a, o):
        ry = other if o == 0 else r
        for i in range(nx):
            arrive(a_rows(a, ry, 1 - c, ((x + nx - i) % nx) * 2, 2), pair(f_sem, a, o, i))

    def far_rows(core):
        return pl.ds(aligned(core * 128, 128), 128)

    def far_send():
        push(a_buf.at[na - 1, other, far_rows(c)], a_far.at[far_rows(c)], pair(far_sem, 0), across)

    def far_wait():
        arrive(a_far.at[far_rows(c)], pair(far_sem, 0))
        push(a_far.at[far_rows(c)], a_far.at[far_rows(c)], pair(far_sem, 1), sibling)
        arrive(a_far.at[far_rows(1 - c)], pair(far_sem, 1))

    chunks = [(a, half, False) for a in range(na) for half in range(HALVES)]
    both = [(na - 1, HALVES - 1)]
    chunks += [(a, half, True) for a, half in both]
    handed = [j for j, (a, half, extra) in enumerate(chunks) if (a, half) not in both]

    def centre_cols(j):
        a, half, extra = chunks[j]
        first = (other if extra else r) * kv
        lanes = pl.ds(half * wide, wide)

        def body(i, carry):
            at = pl.ds(aligned(first + i * STEP, STEP), STEP)
            to = pl.ds(aligned(z * kv + i * STEP, STEP), STEP)
            f = freq[a, at, :]
            f = jnp.concatenate([f] * (wide // 128), axis=1)
            value = ca[a, 0, at, lanes].astype(F32) * (cd[0, at, lanes].astype(F32) - f)
            value = value + ca[a, 1, at, lanes].astype(F32) * (cd[1, at, lanes].astype(F32) - f)
            b_buf[j, to, :] = value.astype(BF16)
            return carry

        lax.fori_loop(0, kv // STEP, body, 0)

    ways = (1, nz - 1)

    def b_part(j, zz, way, d):
        first, count = (way * (kv // 2), kv // 2) if d == far else (0, kv)
        return b_buf.at[j, pl.ds(aligned(zz * kv + first, 64), count), :]

    def b_move(j, way, d):
        ref = b_part(j, (z + (nz - ways[way]) * (d - 1)) % nz, way, d)
        push(ref, ref, pair(b_sem, j, way, d - 1), device(s, (z + ways[way]) % nz, r))

    def launch(j):
        for way in range(2):
            b_move(j, way, 1)

    def hop(j, d):
        for way in range(2):
            arrive(b_part(j, (z + (nz - ways[way]) * d) % nz, way, d), pair(b_sem, j, way, d - 1))
            if d < far:
                b_move(j, way, d + 1)

    def hand_over(j):
        a = chunks[j][0]
        c_send[j] = jnp.dot(a_buf[a, other], b_buf[j], preferred_element_type=F32)
        push(c_send.at[j], c_recv.at[j], pair(c_sem, j), mate)

    def out_lanes(j):
        return pl.ds(chunks[j][1] * wide, wide)

    def keep(j):
        a = chunks[j][0]
        o_buf[a, :, out_lanes(j)] = jnp.dot(a_buf[a, r], b_buf[j], preferred_element_type=F32)

    stores = []

    def store(j):
        a = chunks[j][0]
        copy = pltpu.make_async_copy(o_buf.at[a, :, out_lanes(j)], out_ref.at[a, :, out_lanes(j)], out_sem.at[j])
        copy.start()
        stores.append(copy)

    def finish(j):
        a = chunks[j][0]
        arrive(c_recv.at[j], pair(c_sem, j))
        o_buf[a, :, out_lanes(j)] += c_recv[j]
        store(j)

    centre_rows(0)
    t2_send(0)
    for j in range(2):
        centre_cols(j)
        launch(j)
    centre_cols(2)
    launch(2)
    for a in range(1, na):
        centre_rows(a)
        t2_send(a)
    spreads[z, 0:4, :] = jnp.broadcast_to(jnp.sum(ratio * (1.0 - ratio), axis=1, keepdims=True), (4, 128))
    spreads[z, 4:8, :] = jnp.zeros((4, 128), F32)
    for i in range(1, nz):
        push(spreads.at[z], spreads.at[z], pair(spread_sem, i), device(s, (z + i) % nz, r))
    for j in range(3, len(chunks)):
        centre_cols(j)

    hop(0, 1)
    t2_wait(0)
    g1_send(0, 0)
    g1_send(0, 1)
    hop(1, 1)
    hop(2, 1)
    for a in range(1, na):
        t2_wait(a)
        g1_send(a, 0)
        g1_send(a, 1)
    hop(0, 2)
    hop(1, 2)
    g1_wait(0, 0)
    g2_send(0, 0)
    g1_wait(0, 1)
    g2_send(0, 1)
    hop(2, 2)
    for a in range(1, na):
        for o in range(2):
            g1_wait(a, o)
            g2_send(a, o)
    hop(0, 3)
    launch(3)
    hop(1, 3)
    launch(4)
    hop(2, 3)
    launch(5)
    g2_wait(0, 0)
    f_wait(0, 0)
    hop(0, 4)
    hand_over(0)
    launch(6)
    hop(1, 4)
    hand_over(1)
    g2_wait(1, 0)
    hop(3, 1)
    hop(2, 4)
    f_wait(1, 0)
    hand_over(2)
    hop(4, 1)
    hop(5, 1)
    hop(6, 1)
    g2_wait(0, 1)
    f_wait(0, 1)
    keep(0)
    keep(1)
    hop(3, 2)
    g2_wait(1, 1)
    g2_wait(2, 0)
    f_wait(1, 1)
    keep(2)
    hop(4, 2)
    hop(5, 2)
    g2_wait(2, 1)
    f_wait(2, 0)
    f_wait(2, 1)
    far_send()
    hop(6, 2)
    finish(0)
    hop(3, 3)
    hop(4, 3)
    hop(5, 3)
    far_wait()
    hop(6, 3)
    finish(1)
    hop(3, 4)
    hand_over(3)
    keep(3)
    hop(4, 4)
    hand_over(4)
    keep(4)
    finish(2)
    hop(5, 4)
    hop(6, 4)
    a, lanes = chunks[5][0], out_lanes(5)
    o_buf[a, :, lanes] = jnp.dot(a_buf[a, r], b_buf[5], preferred_element_type=F32)
    o_buf[a, :, lanes] += jnp.dot(a_far[...], b_buf[6], preferred_element_type=F32)
    store(5)

    for i in range(1, nz):
        arrive(spreads.at[(z + nz - i) % nz], pair(spread_sem, i))
    spread = spreads[0]
    for i in range(1, nz):
        spread = spread + spreads[i]
    for a in range(na):
        spread_ref[a:a + 1, :] = jnp.concatenate([spread[a:a + 1, :]] * (cols // 128), axis=1)
    for j in handed[3:]:
        finish(j)

    for copy in sent:
        copy.wait_send()
    for copy in stores:
        copy.wait()


def local(sizes, col_dosage, col_ancestry, row_dosage, row_ancestry):
    ns, nz, nr = sizes
    nx, np_ = ns // 4, ns // 2
    na = col_ancestry.shape[0]
    nv, cols = col_dosage.shape[1:]
    rows = row_dosage.shape[2]
    kv = nv // nr
    tall = 2 * rows
    wide = cols // HALVES
    piece = rows // np_
    chunks = na * HALVES + 1
    far = nz // 2
    dma = pltpu.SemaphoreType.DMA
    total, spread = pl.pallas_call(
        functools.partial(kernel, sizes),
        out_shape=(
            jax.ShapeDtypeStruct((na, tall, cols), F32),
            jax.ShapeDtypeStruct((na, cols), F32),
        ),
        in_specs=[pl.BlockSpec(memory_space=pltpu.HBM)] * 4,
        out_specs=(pl.BlockSpec(memory_space=pl.ANY), pl.BlockSpec(memory_space=pltpu.VMEM)),
        scratch_shapes=[
            pltpu.VMEM(col_dosage.shape, BF16),
            pltpu.VMEM(col_ancestry.shape, BF16),
            pltpu.VMEM(row_dosage.shape, BF16),
            pltpu.VMEM(row_ancestry.shape, BF16),
            pltpu.VMEM((8, nv, 128), F32),
            pltpu.VMEM((2, 8, nv), F32),
            pltpu.VMEM((np_, 8, nv), F32),
            pltpu.VMEM((8, nv), F32),
            pltpu.VMEM((na, nv, 128), F32),
            pltpu.VMEM((nz, 8, 128), F32),
            pltpu.VMEM((2 + 2 * na, rows, nv), BF16),
            pltpu.VMEM((2 + 2 * na, np_, nr, piece, kv), BF16),
            pltpu.VMEM((na, np_, nr, piece, kv), BF16),
            pltpu.VMEM((na, nr, piece, nz * kv), BF16),
            pltpu.VMEM((na, nr, tall, nz * kv), BF16),
            pltpu.VMEM((tall, nz * kv), BF16),
            pltpu.VMEM((chunks, nz * kv, wide), BF16),
            pltpu.VMEM((chunks, tall, wide), F32),
            pltpu.VMEM((chunks, tall, wide), F32),
            pltpu.VMEM((na, tall, cols), F32),
            dma((4,)),
            dma((chunks,)),
            dma((2, 1)),
            dma((2, 2, nx)),
            dma((2, nz)),
            dma((2, np_, nr)),
            dma((2, na, nz)),
            dma((2, na, 2, 2)),
            dma((2, na, 2, nx)),
            dma((2, na, 2, nx)),
            dma((2, 2)),
            dma((2, chunks, 2, far)),
            dma((2, chunks)),
        ],
        compiler_params=pltpu.CompilerParams(
            collective_id=0, has_side_effects=True, vmem_limit_bytes=60 * 1024 * 1024
        ),
    )(col_dosage, col_ancestry, row_dosage, row_ancestry)
    return jnp.transpose(total / spread[:, None, :], (1, 0, 2))


def solution(mesh):
    sizes = (mesh.shape["samp"], mesh.shape["var"], mesh.shape["row"])
    placed = (
        P(None, "var", "samp"),
        P(None, None, "var", "samp"),
        P(None, "var", ("row", "samp")),
        P(None, None, "var", ("row", "samp")),
    )
    return jax.shard_map(
        functools.partial(local, sizes),
        mesh=mesh,
        in_specs=placed,
        out_specs=P(("row", "var"), None, "samp"),
        check_vma=False,
    )
```

```python
import functools

import jax
import jax.numpy as jnp
from jax import lax
from jax.experimental import pallas as pl
from jax.experimental.pallas import tpu as pltpu
from jax.sharding import PartitionSpec as P

MESH = pl.DeviceIdType.MESH
F32 = jnp.float32
BF16 = jnp.bfloat16
HALVES = 2
STEP = 32


def device(s, z, r):
    return {"samp": s, "var": z, "row": r}


def aligned(value, size):
    return pl.multiple_of(value, size)


def kernel(
    sizes,
    cd_hbm,
    ca_hbm,
    rd_hbm,
    ra_hbm,
    out_ref,
    spread_ref,
    cd,
    ca,
    rd,
    ra,
    pst,
    part,
    stat,
    ratios,
    freq,
    spreads,
    turned,
    raw,
    centred,
    hold,
    a_buf,
    a_far,
    b_buf,
    c_send,
    c_recv,
    o_buf,
    in_sem,
    out_sem,
    pair_sem,
    stat_sem,
    spread_sem,
    t1_sem,
    t2_sem,
    g1_sem,
    g2_sem,
    f_sem,
    far_sem,
    b_sem,
    c_sem,
):
    ns, nz, nr = sizes
    nx, np_ = ns // 4, ns // 2
    s, z, r = lax.axis_index("samp"), lax.axis_index("var"), lax.axis_index("row")
    x, h, c = s // 4, (s // 2) % 2, s % 2
    p = s // 2
    other = 1 - r
    na = ca.shape[0]
    nv, cols = cd.shape[1:]
    kv = nv // nr
    wide = cols // HALVES
    piece = rd.shape[2] // np_
    far = nz // 2
    sibling = device(s + 1 - 2 * c, z, r)
    mate = device(s, z, other)
    across = device((x * 2 + 1 - h) * 2 + c, z, other)

    def chip(q):
        return q * 2 + c

    loads = [
        pltpu.make_async_copy(src, dst, in_sem.at[i])
        for i, (src, dst) in enumerate(((cd_hbm, cd), (ca_hbm, ca), (rd_hbm, rd), (ra_hbm, ra)))
    ]
    for load in loads:
        load.start()

    barrier = pltpu.get_barrier_semaphore()

    def greet(who):
        pl.semaphore_signal(barrier, inc=1, device_id=who, device_id_type=MESH)

    greet(sibling)
    for i in range(1, nz):
        greet(device(s, (z + i) % nz, r))
    for i in range(np_):
        for k in range(nr):
            if i or k:
                greet(device(chip((p + i) % np_), z, (r + k) % nr))

    loads[0].wait()
    loads[1].wait()

    def fold(value):
        total = value[:, :128]
        for t in range(1, cols // 128):
            total = total + value[:, t * 128:(t + 1) * 128]
        return total

    def stats(i, carry):
        rows = pl.ds(aligned(i * STEP, STEP), STEP)
        dosage = [cd[k, rows, :].astype(F32) for k in range(2)]
        for a in range(na):
            share = [ca[a, k, rows, :].astype(F32) for k in range(2)]
            pst[a, rows, :] = fold(share[0] + share[1])
            pst[4 + a, rows, :] = fold(share[0] * dosage[0] + share[1] * dosage[1])
        return carry

    lax.fori_loop(0, nv // STEP, stats, 0)
    for a in range(na):
        for k in (a, 4 + a):
            part[c, k:k + 1, :] = jnp.sum(pst[k].T, axis=0, keepdims=True)
    for k in (3, 7):
        part[c, k:k + 1, :] = jnp.ones((1, nv), F32)

    loads[2].wait()
    loads[3].wait()
    for k in range(2):
        turned[k] = rd[k].astype(F32).T.astype(BF16)
        for a in range(na):
            turned[2 + 2 * a + k] = ra[a, k].astype(F32).T.astype(BF16)

    pl.semaphore_wait(barrier, 1 + (nz - 1) + np_ * nr - 1)

    sent = []

    def push(src, dst, sems, who):
        copy = pltpu.make_async_remote_copy(
            src_ref=src, dst_ref=dst, send_sem=sems[0], recv_sem=sems[1], device_id=who, device_id_type=MESH
        )
        copy.start()
        sent.append(copy)

    def pair(ref, *at):
        return ref.at[(0, *at)], ref.at[(1, *at)]

    def arrive(dst, sems):
        pltpu.make_async_copy(dst, dst, sems[1]).wait()

    push(part.at[c], part.at[c], pair(pair_sem, 0), sibling)

    arrive(part.at[1 - c], pair(pair_sem, 0))
    stat[p] = part[0] + part[1]
    for i in range(1, nx):
        push(stat.at[p], stat.at[p], pair(stat_sem, 0, i), device(chip(((x + i) % nx) * 2 + h), z, r))
    for i in range(nx):
        push(stat.at[p], stat.at[p], pair(stat_sem, 1, i), device(chip(((x + i) % nx) * 2 + 1 - h), z, other))

    kinds = (pl.ds(0, 4), pl.ds(4, 2 * na - 2))

    def t1_piece(g, i, k):
        rows = pl.ds(aligned(((p + i) % np_) * piece, piece), piece)
        half = pl.ds(aligned((1 - (r + k) % nr) * kv, kv), kv)
        return turned.at[kinds[g], rows, half], raw.at[kinds[g], p, r]

    for g in range(2):
        pltpu.make_async_copy(*t1_piece(g, 0, 0), t1_sem.at[1, g, 0, 0]).start()
        for i in range(np_):
            for k in range(nr):
                if i or k:
                    push(*t1_piece(g, i, k), pair(t1_sem, g, i, k), device(chip((p + i) % np_), z, (r + k) % nr))

    def t1_wait(g):
        for i in range(np_):
            for k in range(nr):
                arrive(raw.at[kinds[g], (p + np_ - i) % np_, (r + nr - k) % nr], pair(t1_sem, g, i, k))

    for i in range(1, nx):
        arrive(stat.at[((x + nx - i) % nx) * 2 + h], pair(stat_sem, 0, i))
    for i in range(nx):
        arrive(stat.at[((x + nx - i) % nx) * 2 + 1 - h], pair(stat_sem, 1, i))
    total = stat[0]
    for i in range(1, np_):
        total = total + stat[i]
    ratio = total[4:8] / total[0:4]
    ratios[0:4, :] = ratio
    for a in range(na):
        freq[a] = jnp.broadcast_to(ratio[a:a + 1, :], (128, nv)).T

    def centre_rows(a):
        f = ratios[a:a + 1, pl.ds(aligned(other * kv, kv), kv)]
        f = jnp.broadcast_to(f, (piece, kv))[None, None]
        value = raw[2 + 2 * a].astype(F32) * (raw[0].astype(F32) - f)
        value = value + raw[3 + 2 * a].astype(F32) * (raw[1].astype(F32) - f)
        centred[a] = value.astype(BF16)
        hold[a, :, :, pl.ds(aligned(z * kv, kv), kv)] = centred[a, z]

    def hold_from(a, zz):
        return hold.at[a, :, :, pl.ds(aligned(zz * kv, kv), kv)]

    def t2_send(a):
        for i in range(1, nz):
            to = (z + i) % nz
            push(centred.at[a, to], hold_from(a, z), pair(t2_sem, a, i), device(s, to, r))

    def a_rows(a, ry, core, first, count):
        return a_buf.at[a, ry, pl.ds(aligned(core * 128 + first * piece, piece), count * piece), :]

    def t2_wait(a):
        for i in range(1, nz):
            arrive(hold_from(a, (z + nz - i) % nz), pair(t2_sem, a, i))

    def g1_send(a, o):
        ry = r if o == 0 else other
        for k, who in enumerate((mate, across)):
            push(hold.at[a, ry], a_rows(a, ry, c, p, 1), pair(g1_sem, a, o, k), who)

    def g1_wait(a, o):
        ry = other if o == 0 else r
        arrive(a_rows(a, ry, c, p, 1), pair(g1_sem, a, o, 0))
        arrive(a_rows(a, ry, c, x * 2 + 1 - h, 1), pair(g1_sem, a, o, 1))

    def g2_send(a, o):
        ry = other if o == 0 else r
        ref = a_rows(a, ry, c, x * 2, 2)
        for i in range(1, nx):
            push(ref, ref, pair(g2_sem, a, o, i), device(chip(((x + i) % nx) * 2 + h), z, r))
        push(ref, ref, pair(f_sem, a, o, 0), sibling)

    def g2_wait(a, o):
        ry = other if o == 0 else r
        for i in range(1, nx):
            ref = a_rows(a, ry, c, ((x + nx - i) % nx) * 2, 2)
            arrive(ref, pair(g2_sem, a, o, i))
            push(ref, ref, pair(f_sem, a, o, i), sibling)

    def f_wait(a, o):
        ry = other if o == 0 else r
        for i in range(nx):
            arrive(a_rows(a, ry, 1 - c, ((x + nx - i) % nx) * 2, 2), pair(f_sem, a, o, i))

    def far_rows(core):
        return pl.ds(aligned(core * 128, 128), 128)

    def far_send():
        push(a_buf.at[na - 1, other, far_rows(c)], a_far.at[far_rows(c)], pair(far_sem, 0), across)

    def far_wait():
        arrive(a_far.at[far_rows(c)], pair(far_sem, 0))
        push(a_far.at[far_rows(c)], a_far.at[far_rows(c)], pair(far_sem, 1), sibling)
        arrive(a_far.at[far_rows(1 - c)], pair(far_sem, 1))

    chunks = [(a, half, False) for a in range(na) for half in range(HALVES)]
    both = [(na - 1, HALVES - 1)]
    chunks += [(a, half, True) for a, half in both]
    handed = [j for j, (a, half, extra) in enumerate(chunks) if (a, half) not in both]

    def centre_cols(j):
        a, half, extra = chunks[j]
        first = (other if extra else r) * kv
        lanes = pl.ds(half * wide, wide)

        def body(i, carry):
            at = pl.ds(aligned(first + i * STEP, STEP), STEP)
            to = pl.ds(aligned(z * kv + i * STEP, STEP), STEP)
            f = freq[a, at, :]
            f = jnp.concatenate([f] * (wide // 128), axis=1)
            value = ca[a, 0, at, lanes].astype(F32) * (cd[0, at, lanes].astype(F32) - f)
            value = value + ca[a, 1, at, lanes].astype(F32) * (cd[1, at, lanes].astype(F32) - f)
            b_buf[j, to, :] = value.astype(BF16)
            return carry

        lax.fori_loop(0, kv // STEP, body, 0)

    ways = (1, nz - 1)

    def b_part(j, zz, way, d):
        first, count = (way * (kv // 2), kv // 2) if d == far else (0, kv)
        return b_buf.at[j, pl.ds(aligned(zz * kv + first, 64), count), :]

    def b_move(j, way, d):
        ref = b_part(j, (z + (nz - ways[way]) * (d - 1)) % nz, way, d)
        push(ref, ref, pair(b_sem, j, way, d - 1), device(s, (z + ways[way]) % nz, r))

    def launch(j):
        for way in range(2):
            b_move(j, way, 1)

    def hop(j, d):
        for way in range(2):
            arrive(b_part(j, (z + (nz - ways[way]) * d) % nz, way, d), pair(b_sem, j, way, d - 1))
            if d < far:
                b_move(j, way, d + 1)

    def hand_over(j):
        a = chunks[j][0]
        c_send[j] = jnp.dot(a_buf[a, other], b_buf[j], preferred_element_type=F32)
        push(c_send.at[j], c_recv.at[j], pair(c_sem, j), mate)

    def out_lanes(j):
        return pl.ds(chunks[j][1] * wide, wide)

    def keep(j):
        a = chunks[j][0]
        o_buf[a, :, out_lanes(j)] = jnp.dot(a_buf[a, r], b_buf[j], preferred_element_type=F32)

    stores = []

    def store(j):
        a = chunks[j][0]
        copy = pltpu.make_async_copy(o_buf.at[a, :, out_lanes(j)], out_ref.at[a, :, out_lanes(j)], out_sem.at[j])
        copy.start()
        stores.append(copy)

    def finish(j):
        a = chunks[j][0]
        arrive(c_recv.at[j], pair(c_sem, j))
        o_buf[a, :, out_lanes(j)] += c_recv[j]
        store(j)

    def share_spread():
        spreads[z, 0:4, :] = jnp.broadcast_to(jnp.sum(ratio * (1.0 - ratio), axis=1, keepdims=True), (4, 128))
        spreads[z, 4:8, :] = jnp.zeros((4, 128), F32)
        for i in range(1, nz):
            push(spreads.at[z], spreads.at[z], pair(spread_sem, i), device(s, (z + i) % nz, r))

    centre_cols(0)
    launch(0)
    t1_wait(0)
    centre_rows(0)
    t2_send(0)
    for j in range(1, 3):
        centre_cols(j)
        launch(j)
    t1_wait(1)
    for a in range(1, na):
        centre_rows(a)
        t2_send(a)
    share_spread()
    for j in range(3, len(chunks)):
        centre_cols(j)
    hop(0, 1)
    t2_wait(0)
    g1_send(0, 0)
    hop(1, 1)
    hop(2, 1)
    for a in range(1, na):
        t2_wait(a)
        g1_send(a, 0)
    g1_wait(0, 0)
    g2_send(0, 0)
    for a in range(na):
        g1_send(a, 1)
    hop(0, 2)
    hop(1, 2)
    hop(2, 2)
    g1_wait(1, 0)
    g2_send(1, 0)
    hop(0, 3)
    launch(3)
    hop(1, 3)
    hop(2, 3)
    launch(4)
    g2_wait(0, 0)
    g1_wait(2, 0)
    g2_send(2, 0)
    f_wait(0, 0)
    hop(0, 4)
    hand_over(0)
    launch(5)
    hop(1, 4)
    hand_over(1)
    launch(6)
    g1_wait(0, 1)
    g2_send(0, 1)
    hop(3, 1)
    hop(2, 4)
    g2_wait(1, 0)
    f_wait(1, 0)
    hand_over(2)
    hop(4, 1)
    g1_wait(1, 1)
    g2_send(1, 1)
    hop(5, 1)
    hop(6, 1)
    g2_wait(2, 0)
    far_send()
    g1_wait(2, 1)
    g2_send(2, 1)
    hop(3, 2)
    hop(4, 2)
    g2_wait(0, 1)
    hop(5, 2)
    f_wait(0, 1)
    keep(0)
    keep(1)
    hop(6, 2)
    g2_wait(1, 1)
    finish(0)
    f_wait(1, 1)
    keep(2)
    hop(3, 3)
    hop(4, 3)
    g2_wait(2, 1)
    hop(5, 3)
    far_wait()
    hop(6, 3)
    f_wait(2, 0)
    f_wait(2, 1)
    finish(1)
    hop(3, 4)
    hand_over(3)
    keep(3)
    hop(4, 4)
    hand_over(4)
    keep(4)
    finish(2)
    hop(5, 4)
    hop(6, 4)
    a, lanes = chunks[5][0], out_lanes(5)
    o_buf[a, :, lanes] = jnp.dot(a_buf[a, r], b_buf[5], preferred_element_type=F32)
    o_buf[a, :, lanes] += jnp.dot(a_far[...], b_buf[6], preferred_element_type=F32)
    store(5)

    for i in range(1, nz):
        arrive(spreads.at[(z + nz - i) % nz], pair(spread_sem, i))
    spread = spreads[0]
    for i in range(1, nz):
        spread = spread + spreads[i]
    for a in range(na):
        spread_ref[a:a + 1, :] = jnp.concatenate([spread[a:a + 1, :]] * (cols // 128), axis=1)
    for j in handed[3:]:
        finish(j)

    for copy in sent:
        copy.wait_send()
    for copy in stores:
        copy.wait()


def local(sizes, col_dosage, col_ancestry, row_dosage, row_ancestry):
    ns, nz, nr = sizes
    nx, np_ = ns // 4, ns // 2
    na = col_ancestry.shape[0]
    nv, cols = col_dosage.shape[1:]
    rows = row_dosage.shape[2]
    kv = nv // nr
    tall = 2 * rows
    wide = cols // HALVES
    piece = rows // np_
    chunks = na * HALVES + 1
    far = nz // 2
    dma = pltpu.SemaphoreType.DMA
    total, spread = pl.pallas_call(
        functools.partial(kernel, sizes),
        out_shape=(
            jax.ShapeDtypeStruct((na, tall, cols), F32),
            jax.ShapeDtypeStruct((na, cols), F32),
        ),
        in_specs=[pl.BlockSpec(memory_space=pltpu.HBM)] * 4,
        out_specs=(pl.BlockSpec(memory_space=pl.ANY), pl.BlockSpec(memory_space=pltpu.VMEM)),
        scratch_shapes=[
            pltpu.VMEM(col_dosage.shape, BF16),
            pltpu.VMEM(col_ancestry.shape, BF16),
            pltpu.VMEM(row_dosage.shape, BF16),
            pltpu.VMEM(row_ancestry.shape, BF16),
            pltpu.VMEM((8, nv, 128), F32),
            pltpu.VMEM((2, 8, nv), F32),
            pltpu.VMEM((np_, 8, nv), F32),
            pltpu.VMEM((8, nv), F32),
            pltpu.VMEM((na, nv, 128), F32),
            pltpu.VMEM((nz, 8, 128), F32),
            pltpu.VMEM((2 + 2 * na, rows, nv), BF16),
            pltpu.VMEM((2 + 2 * na, np_, nr, piece, kv), BF16),
            pltpu.VMEM((na, np_, nr, piece, kv), BF16),
            pltpu.VMEM((na, nr, piece, nz * kv), BF16),
            pltpu.VMEM((na, nr, tall, nz * kv), BF16),
            pltpu.VMEM((tall, nz * kv), BF16),
            pltpu.VMEM((chunks, nz * kv, wide), BF16),
            pltpu.VMEM((chunks, tall, wide), F32),
            pltpu.VMEM((chunks, tall, wide), F32),
            pltpu.VMEM((na, tall, cols), F32),
            dma((4,)),
            dma((chunks,)),
            dma((2, 1)),
            dma((2, 2, nx)),
            dma((2, nz)),
            dma((2, 2, np_, nr)),
            dma((2, na, nz)),
            dma((2, na, 2, 2)),
            dma((2, na, 2, nx)),
            dma((2, na, 2, nx)),
            dma((2, 2)),
            dma((2, chunks, 2, far)),
            dma((2, chunks)),
        ],
        compiler_params=pltpu.CompilerParams(
            collective_id=0, has_side_effects=True, vmem_limit_bytes=60 * 1024 * 1024
        ),
    )(col_dosage, col_ancestry, row_dosage, row_ancestry)
    return jnp.transpose(total / spread[:, None, :], (1, 0, 2))


def solution(mesh):
    sizes = (mesh.shape["samp"], mesh.shape["var"], mesh.shape["row"])
    placed = (
        P(None, "var", "samp"),
        P(None, None, "var", "samp"),
        P(None, "var", ("row", "samp")),
        P(None, None, "var", ("row", "samp")),
    )
    return jax.shard_map(
        functools.partial(local, sizes),
        mesh=mesh,
        in_specs=placed,
        out_specs=P(("row", "var"), None, "samp"),
        check_vma=False,
    )
```

```python
import functools

import jax
import jax.numpy as jnp
from jax import lax
from jax.experimental import pallas as pl
from jax.experimental.pallas import tpu as pltpu
from jax.sharding import PartitionSpec as P

MESH = pl.DeviceIdType.MESH
F32 = jnp.float32
BF16 = jnp.bfloat16
PARTS = 4
WHOLE = 3
STEP = 32


def device(s, z, r):
    return {"samp": s, "var": z, "row": r}


def aligned(value, size):
    return pl.multiple_of(value, size)


def kernel(
    sizes,
    cd_hbm,
    ca_hbm,
    rd_hbm,
    ra_hbm,
    out_ref,
    spread_ref,
    cd,
    ca,
    rd,
    ra,
    pst,
    part,
    stat,
    ratios,
    freq,
    spreads,
    turned,
    raw,
    centred,
    hold,
    a_buf,
    a_far,
    b_buf,
    c_send,
    c_recv,
    o_buf,
    in_sem,
    out_sem,
    pair_sem,
    stat_sem,
    spread_sem,
    t1_sem,
    t2_sem,
    g1_sem,
    g2_sem,
    f_sem,
    far_sem,
    b_sem,
    c_sem,
):
    ns, nz, nr = sizes
    nx, np_ = ns // 4, ns // 2
    s, z, r = lax.axis_index("samp"), lax.axis_index("var"), lax.axis_index("row")
    x, h, c = s // 4, (s // 2) % 2, s % 2
    p = s // 2
    other = 1 - r
    na = ca.shape[0]
    nv, cols = cd.shape[1:]
    kv = nv // nr
    wide = cols // PARTS
    piece = rd.shape[2] // np_
    far = nz // 2
    sibling = device(s + 1 - 2 * c, z, r)
    mate = device(s, z, other)
    across = device((x * 2 + 1 - h) * 2 + c, z, other)

    def chip(q):
        return q * 2 + c

    loads = [
        pltpu.make_async_copy(src, dst, in_sem.at[i])
        for i, (src, dst) in enumerate(((cd_hbm, cd), (ca_hbm, ca), (rd_hbm, rd), (ra_hbm, ra)))
    ]
    for load in loads:
        load.start()

    barrier = pltpu.get_barrier_semaphore()

    def greet(who):
        pl.semaphore_signal(barrier, inc=1, device_id=who, device_id_type=MESH)

    greet(sibling)
    for i in range(1, nz):
        greet(device(s, (z + i) % nz, r))
    for i in range(np_):
        for k in range(nr):
            if i or k:
                greet(device(chip((p + i) % np_), z, (r + k) % nr))

    loads[0].wait()
    loads[1].wait()

    def fold(value):
        total = value[:, :128]
        for t in range(1, cols // 128):
            total = total + value[:, t * 128:(t + 1) * 128]
        return total

    def stats(i, carry):
        rows = pl.ds(aligned(i * STEP, STEP), STEP)
        dosage = [cd[k, rows, :].astype(F32) for k in range(2)]
        for a in range(na):
            share = [ca[a, k, rows, :].astype(F32) for k in range(2)]
            pst[a, rows, :] = fold(share[0] + share[1])
            pst[4 + a, rows, :] = fold(share[0] * dosage[0] + share[1] * dosage[1])
        return carry

    lax.fori_loop(0, nv // STEP, stats, 0)
    for a in range(na):
        for k in (a, 4 + a):
            part[c, k:k + 1, :] = jnp.sum(pst[k].T, axis=0, keepdims=True)
    for k in (3, 7):
        part[c, k:k + 1, :] = jnp.ones((1, nv), F32)

    loads[2].wait()
    loads[3].wait()
    for k in range(2):
        turned[k] = rd[k].astype(F32).T.astype(BF16)
        for a in range(na):
            turned[2 + 2 * a + k] = ra[a, k].astype(F32).T.astype(BF16)

    pl.semaphore_wait(barrier, 1 + (nz - 1) + np_ * nr - 1)

    sent = []

    def push(src, dst, sems, who):
        copy = pltpu.make_async_remote_copy(
            src_ref=src, dst_ref=dst, send_sem=sems[0], recv_sem=sems[1], device_id=who, device_id_type=MESH
        )
        copy.start()
        sent.append(copy)

    def pair(ref, *at):
        return ref.at[(0, *at)], ref.at[(1, *at)]

    def arrive(dst, sems):
        pltpu.make_async_copy(dst, dst, sems[1]).wait()

    push(part.at[c], part.at[c], pair(pair_sem, 0), sibling)

    arrive(part.at[1 - c], pair(pair_sem, 0))
    stat[p] = part[0] + part[1]
    for i in range(1, nx):
        push(stat.at[p], stat.at[p], pair(stat_sem, 0, i), device(chip(((x + i) % nx) * 2 + h), z, r))
    for i in range(nx):
        push(stat.at[p], stat.at[p], pair(stat_sem, 1, i), device(chip(((x + i) % nx) * 2 + 1 - h), z, other))

    kinds = (pl.ds(0, 4), pl.ds(4, 2 * na - 2))

    def t1_piece(g, i, k):
        rows = pl.ds(aligned(((p + i) % np_) * piece, piece), piece)
        half = pl.ds(aligned((1 - (r + k) % nr) * kv, kv), kv)
        return turned.at[kinds[g], rows, half], raw.at[kinds[g], p, r]

    for g in range(2):
        pltpu.make_async_copy(*t1_piece(g, 0, 0), t1_sem.at[1, g, 0, 0]).start()
        for k in range(nr):
            for i in range(np_):
                if i or k:
                    push(*t1_piece(g, i, k), pair(t1_sem, g, i, k), device(chip((p + i) % np_), z, (r + k) % nr))

    def t1_wait(g, k):
        for i in range(np_):
            arrive(raw.at[kinds[g], (p + np_ - i) % np_, (r + nr - k) % nr], pair(t1_sem, g, i, k))

    for i in range(1, nx):
        arrive(stat.at[((x + nx - i) % nx) * 2 + h], pair(stat_sem, 0, i))
    for i in range(nx):
        arrive(stat.at[((x + nx - i) % nx) * 2 + 1 - h], pair(stat_sem, 1, i))
    total = stat[0]
    for i in range(1, np_):
        total = total + stat[i]
    ratio = total[4:8] / total[0:4]
    ratios[0:4, :] = ratio
    for a in range(na):
        freq[a] = jnp.broadcast_to(ratio[a:a + 1, :], (128, nv)).T

    def centre_rows(a, o):
        ry = r if o == 0 else other
        f = ratios[a:a + 1, pl.ds(aligned(other * kv, kv), kv)]
        f = jnp.broadcast_to(f, (piece, kv))[None]
        value = raw[2 + 2 * a, :, ry].astype(F32) * (raw[0, :, ry].astype(F32) - f)
        value = value + raw[3 + 2 * a, :, ry].astype(F32) * (raw[1, :, ry].astype(F32) - f)
        centred[a, o] = value.astype(BF16)
        hold[a, o, :, pl.ds(aligned(z * kv, kv), kv)] = centred[a, o, z]

    def hold_from(a, o, zz):
        return hold.at[a, o, :, pl.ds(aligned(zz * kv, kv), kv)]

    def t2_send(a, o):
        for i in range(1, nz):
            to = (z + i) % nz
            push(centred.at[a, o, to], hold_from(a, o, z), pair(t2_sem, a, o, i), device(s, to, r))

    def a_rows(a, ry, core, first, count):
        return a_buf.at[a, ry, pl.ds(aligned(core * 128 + first * piece, piece), count * piece), :]

    def t2_wait(a, o):
        for i in range(1, nz):
            arrive(hold_from(a, o, (z + nz - i) % nz), pair(t2_sem, a, o, i))

    def g1_send(a, o):
        ry = r if o == 0 else other
        for k, who in enumerate((mate, across)):
            push(hold.at[a, o], a_rows(a, ry, c, p, 1), pair(g1_sem, a, o, k), who)

    def g1_wait(a, o):
        ry = other if o == 0 else r
        arrive(a_rows(a, ry, c, p, 1), pair(g1_sem, a, o, 0))
        arrive(a_rows(a, ry, c, x * 2 + 1 - h, 1), pair(g1_sem, a, o, 1))

    def g2_send(a, o):
        ry = other if o == 0 else r
        ref = a_rows(a, ry, c, x * 2, 2)
        for i in range(1, nx):
            push(ref, ref, pair(g2_sem, a, o, i), device(chip(((x + i) % nx) * 2 + h), z, r))
        push(ref, ref, pair(f_sem, a, o, 0), sibling)

    def g2_wait(a, o):
        ry = other if o == 0 else r
        for i in range(1, nx):
            ref = a_rows(a, ry, c, ((x + nx - i) % nx) * 2, 2)
            arrive(ref, pair(g2_sem, a, o, i))
            push(ref, ref, pair(f_sem, a, o, i), sibling)

    def f_wait(a, o):
        ry = other if o == 0 else r
        for i in range(nx):
            arrive(a_rows(a, ry, 1 - c, ((x + nx - i) % nx) * 2, 2), pair(f_sem, a, o, i))

    def far_rows(core):
        return pl.ds(aligned(core * 128, 128), 128)

    def far_send():
        push(a_buf.at[na - 1, other, far_rows(c)], a_far.at[far_rows(c)], pair(far_sem, 0), across)

    def far_wait():
        arrive(a_far.at[far_rows(c)], pair(far_sem, 0))
        push(a_far.at[far_rows(c)], a_far.at[far_rows(c)], pair(far_sem, 1), sibling)
        arrive(a_far.at[far_rows(1 - c)], pair(far_sem, 1))

    chunks = [(a, half, False) for a in range(na) for half in range(PARTS)]
    chunks += [(na - 1, PARTS - 1 - i, True) for i in range(WHOLE)]

    def centre_cols(j):
        a, half, extra = chunks[j]
        first = (other if extra else r) * kv
        lanes = pl.ds(half * wide, wide)

        def body(i, carry):
            at = pl.ds(aligned(first + i * STEP, STEP), STEP)
            to = pl.ds(aligned(z * kv + i * STEP, STEP), STEP)
            f = freq[a, at, :]
            f = jnp.concatenate([f] * (wide // 128), axis=1)
            value = ca[a, 0, at, lanes].astype(F32) * (cd[0, at, lanes].astype(F32) - f)
            value = value + ca[a, 1, at, lanes].astype(F32) * (cd[1, at, lanes].astype(F32) - f)
            b_buf[j, to, :] = value.astype(BF16)
            return carry

        lax.fori_loop(0, kv // STEP, body, 0)

    ways = (1, nz - 1)

    def b_part(j, zz, way, d):
        first, count = (way * (kv // 2), kv // 2) if d == far else (0, kv)
        return b_buf.at[j, pl.ds(aligned(zz * kv + first, 64), count), :]

    def b_move(j, way, d):
        ref = b_part(j, (z + (nz - ways[way]) * (d - 1)) % nz, way, d)
        push(ref, ref, pair(b_sem, j, way, d - 1), device(s, (z + ways[way]) % nz, r))

    def launch(j):
        for way in range(2):
            b_move(j, way, 1)

    def hop(j, d):
        for way in range(2):
            arrive(b_part(j, (z + (nz - ways[way]) * d) % nz, way, d), pair(b_sem, j, way, d - 1))
            if d < far:
                b_move(j, way, d + 1)

    def hand_over(j):
        a = chunks[j][0]
        c_send[j] = jnp.dot(a_buf[a, other], b_buf[j], preferred_element_type=F32)
        push(c_send.at[j], c_recv.at[j], pair(c_sem, j), mate)

    def out_lanes(j):
        return pl.ds(chunks[j][1] * wide, wide)

    def keep(j):
        a = chunks[j][0]
        o_buf[a, :, out_lanes(j)] = jnp.dot(a_buf[a, r], b_buf[j], preferred_element_type=F32)

    stores = []

    def both(j, extra):
        a = chunks[j][0]
        value = jnp.dot(a_buf[a, r], b_buf[j], preferred_element_type=F32)
        o_buf[a, :, out_lanes(j)] = value + jnp.dot(a_far[...], b_buf[extra], preferred_element_type=F32)
        store(j)

    def store(j):
        a = chunks[j][0]
        copy = pltpu.make_async_copy(o_buf.at[a, :, out_lanes(j)], out_ref.at[a, :, out_lanes(j)], out_sem.at[j])
        copy.start()
        stores.append(copy)

    def finish(j):
        a = chunks[j][0]
        arrive(c_recv.at[j], pair(c_sem, j))
        o_buf[a, :, out_lanes(j)] += c_recv[j]
        store(j)

    def share_spread():
        spreads[z, 0:4, :] = jnp.broadcast_to(jnp.sum(ratio * (1.0 - ratio), axis=1, keepdims=True), (4, 128))
        spreads[z, 4:8, :] = jnp.zeros((4, 128), F32)
        for i in range(1, nz):
            push(spreads.at[z], spreads.at[z], pair(spread_sem, i), device(s, (z + i) % nz, r))

    centre_cols(0)
    launch(0)
    centre_cols(1)
    launch(1)
    centre_cols(2)
    launch(2)
    share_spread()
    t1_wait(0, 0)
    centre_rows(0, 0)
    t2_send(0, 0)
    centre_cols(3)
    launch(3)
    t1_wait(1, 0)
    centre_rows(1, 0)
    t2_send(1, 0)
    hop(0, 1)
    centre_rows(2, 0)
    t2_send(2, 0)
    hop(1, 1)
    t1_wait(0, 1)
    centre_rows(0, 1)
    t2_send(0, 1)
    hop(2, 1)
    t1_wait(1, 1)
    centre_rows(1, 1)
    t2_send(1, 1)
    centre_rows(2, 1)
    t2_send(2, 1)
    hop(3, 1)
    hop(0, 2)
    t2_wait(0, 0)
    g1_send(0, 0)
    hop(1, 2)
    t2_wait(1, 0)
    g1_send(1, 0)
    hop(2, 2)
    t2_wait(2, 0)
    g1_send(2, 0)
    g1_wait(0, 0)
    g2_send(0, 0)
    centre_cols(4)
    launch(4)
    t2_wait(0, 1)
    g1_send(0, 1)
    centre_cols(5)
    launch(5)
    hop(3, 2)
    g1_wait(1, 0)
    g2_send(1, 0)
    hop(0, 3)
    t2_wait(1, 1)
    g1_send(1, 1)
    centre_cols(6)
    launch(6)
    g1_wait(2, 0)
    g2_send(2, 0)
    hop(1, 3)
    hop(2, 3)
    t2_wait(2, 1)
    g1_send(2, 1)
    centre_cols(7)
    launch(7)
    hop(4, 1)
    g1_wait(0, 1)
    g2_send(0, 1)
    hop(5, 1)
    hop(3, 3)
    g1_wait(1, 1)
    g2_send(1, 1)
    hop(0, 4)
    g2_wait(0, 0)
    centre_cols(8)
    launch(8)
    hop(1, 4)
    hop(6, 1)
    hop(2, 4)
    g1_wait(2, 1)
    g2_send(2, 1)
    centre_cols(11)
    launch(11)
    f_wait(0, 0)
    hand_over(0)
    hand_over(1)
    hand_over(2)
    hop(4, 2)
    g2_wait(1, 0)
    hop(5, 2)
    hop(3, 4)
    hand_over(3)
    centre_cols(12)
    launch(12)
    hop(7, 1)
    hop(8, 1)
    f_wait(1, 0)
    hop(6, 2)
    hop(11, 1)
    g2_wait(2, 0)
    far_send()
    hop(4, 3)
    hop(5, 3)
    f_wait(2, 0)
    hop(12, 1)
    hop(7, 2)
    g2_wait(0, 1)
    hop(8, 2)
    hop(6, 3)
    f_wait(0, 1)
    keep(0)
    centre_cols(10)
    launch(10)
    hop(11, 2)
    hop(4, 4)
    hand_over(4)
    hop(5, 4)
    hand_over(5)
    centre_cols(13)
    launch(13)
    g2_wait(1, 1)
    centre_cols(9)
    launch(9)
    hop(7, 3)
    hop(12, 2)
    keep(1)
    hop(8, 3)
    hop(6, 4)
    hand_over(6)
    f_wait(1, 1)
    g2_wait(2, 1)
    hop(10, 1)
    far_wait()
    keep(2)
    hop(11, 3)
    keep(3)
    keep(4)
    centre_cols(14)
    launch(14)
    f_wait(2, 1)
    hop(13, 1)
    keep(5)
    hop(9, 1)
    keep(6)
    hop(7, 4)
    hand_over(7)
    keep(7)
    hop(12, 3)
    hop(8, 4)
    hand_over(8)
    keep(8)
    hop(10, 2)
    finish(0)
    hop(11, 4)
    finish(1)
    finish(2)
    finish(3)
    finish(4)
    hop(14, 1)
    hop(13, 2)
    hop(9, 2)
    hop(12, 4)
    both(11, 12)
    finish(5)
    hop(10, 3)
    hop(14, 2)
    hop(13, 3)
    finish(6)
    hop(9, 3)
    hop(10, 4)
    hop(14, 3)
    hop(13, 4)
    both(10, 13)
    finish(7)
    hop(9, 4)
    hop(14, 4)
    both(9, 14)
    finish(8)

    for i in range(1, nz):
        arrive(spreads.at[(z + nz - i) % nz], pair(spread_sem, i))
    spread = spreads[0]
    for i in range(1, nz):
        spread = spread + spreads[i]
    for a in range(na):
        spread_ref[a:a + 1, :] = jnp.concatenate([spread[a:a + 1, :]] * (cols // 128), axis=1)
    for copy in sent:
        copy.wait_send()
    for copy in stores:
        copy.wait()


def local(sizes, col_dosage, col_ancestry, row_dosage, row_ancestry):
    ns, nz, nr = sizes
    nx, np_ = ns // 4, ns // 2
    na = col_ancestry.shape[0]
    nv, cols = col_dosage.shape[1:]
    rows = row_dosage.shape[2]
    kv = nv // nr
    tall = 2 * rows
    wide = cols // PARTS
    piece = rows // np_
    chunks = na * PARTS + WHOLE
    far = nz // 2
    dma = pltpu.SemaphoreType.DMA
    total, spread = pl.pallas_call(
        functools.partial(kernel, sizes),
        out_shape=(
            jax.ShapeDtypeStruct((na, tall, cols), F32),
            jax.ShapeDtypeStruct((na, cols), F32),
        ),
        in_specs=[pl.BlockSpec(memory_space=pltpu.HBM)] * 4,
        out_specs=(pl.BlockSpec(memory_space=pl.ANY), pl.BlockSpec(memory_space=pltpu.VMEM)),
        scratch_shapes=[
            pltpu.VMEM(col_dosage.shape, BF16),
            pltpu.VMEM(col_ancestry.shape, BF16),
            pltpu.VMEM(row_dosage.shape, BF16),
            pltpu.VMEM(row_ancestry.shape, BF16),
            pltpu.VMEM((8, nv, 128), F32),
            pltpu.VMEM((2, 8, nv), F32),
            pltpu.VMEM((np_, 8, nv), F32),
            pltpu.VMEM((8, nv), F32),
            pltpu.VMEM((na, nv, 128), F32),
            pltpu.VMEM((nz, 8, 128), F32),
            pltpu.VMEM((2 + 2 * na, rows, nv), BF16),
            pltpu.VMEM((2 + 2 * na, np_, nr, piece, kv), BF16),
            pltpu.VMEM((na, nr, np_, piece, kv), BF16),
            pltpu.VMEM((na, nr, piece, nz * kv), BF16),
            pltpu.VMEM((na, nr, tall, nz * kv), BF16),
            pltpu.VMEM((tall, nz * kv), BF16),
            pltpu.VMEM((chunks, nz * kv, wide), BF16),
            pltpu.VMEM((chunks, tall, wide), F32),
            pltpu.VMEM((chunks, tall, wide), F32),
            pltpu.VMEM((na, tall, cols), F32),
            dma((4,)),
            dma((chunks,)),
            dma((2, 1)),
            dma((2, 2, nx)),
            dma((2, nz)),
            dma((2, 2, np_, nr)),
            dma((2, na, 2, nz)),
            dma((2, na, 2, 2)),
            dma((2, na, 2, nx)),
            dma((2, na, 2, nx)),
            dma((2, 2)),
            dma((2, chunks, 2, far)),
            dma((2, chunks)),
        ],
        compiler_params=pltpu.CompilerParams(
            collective_id=0, has_side_effects=True, vmem_limit_bytes=60 * 1024 * 1024
        ),
    )(col_dosage, col_ancestry, row_dosage, row_ancestry)
    return jnp.transpose(total / spread[:, None, :], (1, 0, 2))


def solution(mesh):
    sizes = (mesh.shape["samp"], mesh.shape["var"], mesh.shape["row"])
    placed = (
        P(None, "var", "samp"),
        P(None, None, "var", "samp"),
        P(None, "var", ("row", "samp")),
        P(None, None, "var", ("row", "samp")),
    )
    return jax.shard_map(
        functools.partial(local, sizes),
        mesh=mesh,
        in_specs=placed,
        out_specs=P(("row", "var"), None, "samp"),
        check_vma=False,
    )
```

```python
import functools

import jax
import jax.numpy as jnp
from jax import lax
from jax.experimental import pallas as pl
from jax.experimental.pallas import tpu as pltpu
from jax.sharding import PartitionSpec as P

MESH = pl.DeviceIdType.MESH
F32 = jnp.float32
BF16 = jnp.bfloat16
PARTS = 4
WHOLE = 3
STEP = 32


def device(s, z, r):
    return {"samp": s, "var": z, "row": r}


def aligned(value, size):
    return pl.multiple_of(value, size)


def kernel(
    sizes,
    cd_hbm,
    ca_hbm,
    rd_hbm,
    ra_hbm,
    o_buf,
    spread_ref,
    cd,
    ca,
    rd,
    ra,
    pst,
    part,
    stat,
    ratios,
    freq,
    spreads,
    turned,
    raw,
    centred,
    hold,
    a_buf,
    a_far,
    b_buf,
    c_send,
    c_recv,
    in_sem,
    pair_sem,
    stat_sem,
    spread_sem,
    t1_sem,
    t2_sem,
    g1_sem,
    g2_sem,
    f_sem,
    far_sem,
    b_sem,
    c_sem,
):
    ns, nz, nr = sizes
    nx, np_ = ns // 4, ns // 2
    s, z, r = lax.axis_index("samp"), lax.axis_index("var"), lax.axis_index("row")
    x, h, c = s // 4, (s // 2) % 2, s % 2
    p = s // 2
    other = 1 - r
    na = ca.shape[0]
    nv, cols = cd.shape[1:]
    kv = nv // nr
    wide = cols // PARTS
    piece = rd.shape[2] // np_
    far = nz // 2
    sibling = device(s + 1 - 2 * c, z, r)
    mate = device(s, z, other)
    across = device((x * 2 + 1 - h) * 2 + c, z, other)

    def chip(q):
        return q * 2 + c

    loads = [
        pltpu.make_async_copy(src, dst, in_sem.at[i])
        for i, (src, dst) in enumerate(((cd_hbm, cd), (ca_hbm, ca), (rd_hbm, rd), (ra_hbm, ra)))
    ]
    for load in loads:
        load.start()

    barrier = pltpu.get_barrier_semaphore()

    def greet(who):
        pl.semaphore_signal(barrier, inc=1, device_id=who, device_id_type=MESH)

    greet(sibling)
    for i in range(1, nz):
        greet(device(s, (z + i) % nz, r))
    for i in range(np_):
        for k in range(nr):
            if i or k:
                greet(device(chip((p + i) % np_), z, (r + k) % nr))

    loads[0].wait()
    loads[1].wait()

    def fold(value):
        total = value[:, :128]
        for t in range(1, cols // 128):
            total = total + value[:, t * 128:(t + 1) * 128]
        return total

    def stats(i, carry):
        rows = pl.ds(aligned(i * STEP, STEP), STEP)
        dosage = [cd[k, rows, :].astype(F32) for k in range(2)]
        for a in range(na):
            share = [ca[a, k, rows, :].astype(F32) for k in range(2)]
            pst[a, rows, :] = fold(share[0] + share[1])
            pst[4 + a, rows, :] = fold(share[0] * dosage[0] + share[1] * dosage[1])
        return carry

    lax.fori_loop(0, nv // STEP, stats, 0)
    for a in range(na):
        for k in (a, 4 + a):
            part[c, k:k + 1, :] = jnp.sum(pst[k].T, axis=0, keepdims=True)
    for k in (3, 7):
        part[c, k:k + 1, :] = jnp.ones((1, nv), F32)

    loads[2].wait()
    loads[3].wait()
    for k in range(2):
        turned[k] = rd[k].astype(F32).T.astype(BF16)
        for a in range(na):
            turned[2 + 2 * a + k] = ra[a, k].astype(F32).T.astype(BF16)

    pl.semaphore_wait(barrier, 1 + (nz - 1) + np_ * nr - 1)

    sent = []

    def push(src, dst, sems, who):
        copy = pltpu.make_async_remote_copy(
            src_ref=src, dst_ref=dst, send_sem=sems[0], recv_sem=sems[1], device_id=who, device_id_type=MESH
        )
        copy.start()
        sent.append(copy)

    def pair(ref, *at):
        return ref.at[(0, *at)], ref.at[(1, *at)]

    def arrive(dst, sems):
        pltpu.make_async_copy(dst, dst, sems[1]).wait()

    push(part.at[c], part.at[c], pair(pair_sem, 0), sibling)

    arrive(part.at[1 - c], pair(pair_sem, 0))
    stat[p] = part[0] + part[1]
    for i in range(1, nx):
        push(stat.at[p], stat.at[p], pair(stat_sem, 0, i), device(chip(((x + i) % nx) * 2 + h), z, r))
    for i in range(nx):
        push(stat.at[p], stat.at[p], pair(stat_sem, 1, i), device(chip(((x + i) % nx) * 2 + 1 - h), z, other))

    kinds = (pl.ds(0, 4), pl.ds(4, 2 * na - 2))

    def t1_piece(g, i, k):
        rows = pl.ds(aligned(((p + i) % np_) * piece, piece), piece)
        half = pl.ds(aligned((1 - (r + k) % nr) * kv, kv), kv)
        return turned.at[kinds[g], rows, half], raw.at[kinds[g], p, r]

    for g in range(2):
        pltpu.make_async_copy(*t1_piece(g, 0, 0), t1_sem.at[1, g, 0, 0]).start()
        for k in range(nr):
            for i in range(np_):
                if i or k:
                    push(*t1_piece(g, i, k), pair(t1_sem, g, i, k), device(chip((p + i) % np_), z, (r + k) % nr))

    def t1_wait(g, k):
        for i in range(np_):
            arrive(raw.at[kinds[g], (p + np_ - i) % np_, (r + nr - k) % nr], pair(t1_sem, g, i, k))

    for i in range(1, nx):
        arrive(stat.at[((x + nx - i) % nx) * 2 + h], pair(stat_sem, 0, i))
    for i in range(nx):
        arrive(stat.at[((x + nx - i) % nx) * 2 + 1 - h], pair(stat_sem, 1, i))
    total = stat[0]
    for i in range(1, np_):
        total = total + stat[i]
    ratio = total[4:8] / total[0:4]
    ratios[0:4, :] = ratio
    for a in range(na):
        freq[a] = jnp.broadcast_to(ratio[a:a + 1, :], (128, nv)).T

    def centre_rows(a, o):
        ry = r if o == 0 else other
        f = ratios[a:a + 1, pl.ds(aligned(other * kv, kv), kv)]
        f = jnp.broadcast_to(f, (piece, kv))[None]
        value = raw[2 + 2 * a, :, ry].astype(F32) * (raw[0, :, ry].astype(F32) - f)
        value = value + raw[3 + 2 * a, :, ry].astype(F32) * (raw[1, :, ry].astype(F32) - f)
        centred[a, o] = value.astype(BF16)
        hold[a, o, :, pl.ds(aligned(z * kv, kv), kv)] = centred[a, o, z]

    def hold_from(a, o, zz):
        return hold.at[a, o, :, pl.ds(aligned(zz * kv, kv), kv)]

    def t2_send(a, o):
        for i in range(1, nz):
            to = (z + i) % nz
            push(centred.at[a, o, to], hold_from(a, o, z), pair(t2_sem, a, o, i), device(s, to, r))

    def a_rows(a, ry, core, first, count):
        return a_buf.at[a, ry, pl.ds(aligned(core * 128 + first * piece, piece), count * piece), :]

    def t2_wait(a, o):
        for i in range(1, nz):
            arrive(hold_from(a, o, (z + nz - i) % nz), pair(t2_sem, a, o, i))

    def g1_send(a, o):
        ry = r if o == 0 else other
        for k, who in enumerate((mate, across)):
            push(hold.at[a, o], a_rows(a, ry, c, p, 1), pair(g1_sem, a, o, k), who)

    def g1_wait(a, o):
        ry = other if o == 0 else r
        arrive(a_rows(a, ry, c, p, 1), pair(g1_sem, a, o, 0))
        arrive(a_rows(a, ry, c, x * 2 + 1 - h, 1), pair(g1_sem, a, o, 1))

    def g2_send(a, o):
        ry = other if o == 0 else r
        ref = a_rows(a, ry, c, x * 2, 2)
        for i in range(1, nx):
            push(ref, ref, pair(g2_sem, a, o, i), device(chip(((x + i) % nx) * 2 + h), z, r))
        push(ref, ref, pair(f_sem, a, o, 0), sibling)

    def g2_wait(a, o):
        ry = other if o == 0 else r
        for i in range(1, nx):
            ref = a_rows(a, ry, c, ((x + nx - i) % nx) * 2, 2)
            arrive(ref, pair(g2_sem, a, o, i))
            push(ref, ref, pair(f_sem, a, o, i), sibling)

    def f_wait(a, o):
        ry = other if o == 0 else r
        for i in range(nx):
            arrive(a_rows(a, ry, 1 - c, ((x + nx - i) % nx) * 2, 2), pair(f_sem, a, o, i))

    def far_rows(core):
        return pl.ds(aligned(core * 128, 128), 128)

    def far_send():
        push(a_buf.at[na - 1, other, far_rows(c)], a_far.at[far_rows(c)], pair(far_sem, 0), across)

    def far_wait():
        arrive(a_far.at[far_rows(c)], pair(far_sem, 0))
        push(a_far.at[far_rows(c)], a_far.at[far_rows(c)], pair(far_sem, 1), sibling)
        arrive(a_far.at[far_rows(1 - c)], pair(far_sem, 1))

    chunks = [(a, half, False) for a in range(na) for half in range(PARTS)]
    chunks += [(na - 1, PARTS - 1 - i, True) for i in range(WHOLE)]

    def centre_cols(j):
        a, half, extra = chunks[j]
        first = (other if extra else r) * kv
        lanes = pl.ds(half * wide, wide)

        def body(i, carry):
            at = pl.ds(aligned(first + i * STEP, STEP), STEP)
            to = pl.ds(aligned(z * kv + i * STEP, STEP), STEP)
            f = freq[a, at, :]
            f = jnp.concatenate([f] * (wide // 128), axis=1)
            value = ca[a, 0, at, lanes].astype(F32) * (cd[0, at, lanes].astype(F32) - f)
            value = value + ca[a, 1, at, lanes].astype(F32) * (cd[1, at, lanes].astype(F32) - f)
            b_buf[j, to, :] = value.astype(BF16)
            return carry

        lax.fori_loop(0, kv // STEP, body, 0)

    ways = (1, nz - 1)

    def b_part(j, zz, way, d):
        first, count = (way * (kv // 2), kv // 2) if d == far else (0, kv)
        return b_buf.at[j, pl.ds(aligned(zz * kv + first, 64), count), :]

    def b_move(j, way, d):
        ref = b_part(j, (z + (nz - ways[way]) * (d - 1)) % nz, way, d)
        push(ref, ref, pair(b_sem, j, way, d - 1), device(s, (z + ways[way]) % nz, r))

    def launch(j):
        for way in range(2):
            b_move(j, way, 1)

    def hop(j, d):
        for way in range(2):
            arrive(b_part(j, (z + (nz - ways[way]) * d) % nz, way, d), pair(b_sem, j, way, d - 1))
            if d < far:
                b_move(j, way, d + 1)

    def hand_over(j):
        a = chunks[j][0]
        c_send[j] = jnp.dot(a_buf[a, other], b_buf[j], preferred_element_type=F32)
        push(c_send.at[j], c_recv.at[j], pair(c_sem, j), mate)

    def out_lanes(j):
        return pl.ds(chunks[j][1] * wide, wide)

    def keep(j):
        a = chunks[j][0]
        o_buf[a, :, out_lanes(j)] = jnp.dot(a_buf[a, r], b_buf[j], preferred_element_type=F32)

    def both(j, extra):
        a = chunks[j][0]
        value = jnp.dot(a_buf[a, r], b_buf[j], preferred_element_type=F32)
        o_buf[a, :, out_lanes(j)] = value + jnp.dot(a_far[...], b_buf[extra], preferred_element_type=F32)

    def finish(j):
        a = chunks[j][0]
        arrive(c_recv.at[j], pair(c_sem, j))
        o_buf[a, :, out_lanes(j)] += c_recv[j]

    def share_spread():
        spreads[z, 0:4, :] = jnp.broadcast_to(jnp.sum(ratio * (1.0 - ratio), axis=1, keepdims=True), (4, 128))
        spreads[z, 4:8, :] = jnp.zeros((4, 128), F32)
        for i in range(1, nz):
            push(spreads.at[z], spreads.at[z], pair(spread_sem, i), device(s, (z + i) % nz, r))

    centre_cols(0)
    launch(0)
    centre_cols(1)
    launch(1)
    centre_cols(2)
    launch(2)
    share_spread()
    t1_wait(0, 0)
    centre_rows(0, 0)
    t2_send(0, 0)
    centre_cols(3)
    launch(3)
    t1_wait(1, 0)
    centre_rows(1, 0)
    t2_send(1, 0)
    hop(0, 1)
    centre_rows(2, 0)
    t2_send(2, 0)
    hop(1, 1)
    t1_wait(0, 1)
    centre_rows(0, 1)
    t2_send(0, 1)
    hop(2, 1)
    t1_wait(1, 1)
    centre_rows(1, 1)
    t2_send(1, 1)
    centre_rows(2, 1)
    t2_send(2, 1)
    hop(3, 1)
    hop(0, 2)
    t2_wait(0, 0)
    g1_send(0, 0)
    hop(1, 2)
    t2_wait(1, 0)
    g1_send(1, 0)
    hop(2, 2)
    t2_wait(2, 0)
    g1_send(2, 0)
    g1_wait(0, 0)
    g2_send(0, 0)
    centre_cols(4)
    launch(4)
    t2_wait(0, 1)
    g1_send(0, 1)
    centre_cols(5)
    launch(5)
    hop(3, 2)
    g1_wait(1, 0)
    g2_send(1, 0)
    hop(0, 3)
    t2_wait(1, 1)
    g1_send(1, 1)
    centre_cols(6)
    launch(6)
    g1_wait(2, 0)
    g2_send(2, 0)
    hop(1, 3)
    hop(2, 3)
    t2_wait(2, 1)
    g1_send(2, 1)
    centre_cols(7)
    launch(7)
    hop(4, 1)
    g1_wait(0, 1)
    g2_send(0, 1)
    hop(5, 1)
    hop(3, 3)
    g1_wait(1, 1)
    g2_send(1, 1)
    hop(0, 4)
    g2_wait(0, 0)
    centre_cols(8)
    launch(8)
    hop(1, 4)
    hop(6, 1)
    hop(2, 4)
    g1_wait(2, 1)
    g2_send(2, 1)
    centre_cols(11)
    launch(11)
    f_wait(0, 0)
    hand_over(0)
    hand_over(1)
    hand_over(2)
    hop(4, 2)
    g2_wait(1, 0)
    hop(5, 2)
    hop(3, 4)
    hand_over(3)
    centre_cols(12)
    launch(12)
    hop(7, 1)
    hop(8, 1)
    f_wait(1, 0)
    hop(6, 2)
    hop(11, 1)
    g2_wait(2, 0)
    far_send()
    hop(4, 3)
    hop(5, 3)
    f_wait(2, 0)
    hop(12, 1)
    hop(7, 2)
    g2_wait(0, 1)
    hop(8, 2)
    hop(6, 3)
    f_wait(0, 1)
    keep(0)
    centre_cols(10)
    launch(10)
    hop(11, 2)
    hop(4, 4)
    hand_over(4)
    hop(5, 4)
    hand_over(5)
    centre_cols(13)
    launch(13)
    g2_wait(1, 1)
    centre_cols(9)
    launch(9)
    hop(7, 3)
    hop(12, 2)
    keep(1)
    hop(8, 3)
    hop(6, 4)
    hand_over(6)
    f_wait(1, 1)
    g2_wait(2, 1)
    hop(10, 1)
    far_wait()
    keep(2)
    hop(11, 3)
    keep(3)
    keep(4)
    centre_cols(14)
    launch(14)
    f_wait(2, 1)
    hop(13, 1)
    keep(5)
    hop(9, 1)
    keep(6)
    hop(7, 4)
    hand_over(7)
    keep(7)
    hop(12, 3)
    hop(8, 4)
    hand_over(8)
    keep(8)
    hop(10, 2)
    finish(0)
    hop(11, 4)
    finish(1)
    finish(2)
    finish(3)
    finish(4)
    hop(14, 1)
    hop(13, 2)
    hop(9, 2)
    hop(12, 4)
    both(11, 12)
    finish(5)
    hop(10, 3)
    hop(14, 2)
    hop(13, 3)
    finish(6)
    hop(9, 3)
    hop(10, 4)
    hop(14, 3)
    hop(13, 4)
    both(10, 13)
    finish(7)
    hop(9, 4)
    hop(14, 4)
    both(9, 14)
    finish(8)

    for i in range(1, nz):
        arrive(spreads.at[(z + nz - i) % nz], pair(spread_sem, i))
    spread = spreads[0]
    for i in range(1, nz):
        spread = spread + spreads[i]
    for a in range(na):
        spread_ref[a:a + 1, :] = jnp.concatenate([spread[a:a + 1, :]] * (cols // 128), axis=1)
    for copy in sent:
        copy.wait_send()


def local(sizes, col_dosage, col_ancestry, row_dosage, row_ancestry):
    ns, nz, nr = sizes
    nx, np_ = ns // 4, ns // 2
    na = col_ancestry.shape[0]
    nv, cols = col_dosage.shape[1:]
    rows = row_dosage.shape[2]
    kv = nv // nr
    tall = 2 * rows
    wide = cols // PARTS
    piece = rows // np_
    chunks = na * PARTS + WHOLE
    far = nz // 2
    dma = pltpu.SemaphoreType.DMA
    args = (col_dosage, col_ancestry, row_dosage, row_ancestry)
    args = [pltpu.with_memory_space_constraint(v, pltpu.HBM) for v in args]
    total, spread = pl.pallas_call(
        functools.partial(kernel, sizes),
        out_shape=(
            pltpu.VMEM((na, tall, cols), F32),
            jax.ShapeDtypeStruct((na, cols), F32),
        ),
        in_specs=[pl.BlockSpec(memory_space=pltpu.HBM)] * 4,
        out_specs=(pl.BlockSpec(memory_space=pltpu.VMEM), pl.BlockSpec(memory_space=pltpu.VMEM)),
        scratch_shapes=[
            pltpu.VMEM(col_dosage.shape, BF16),
            pltpu.VMEM(col_ancestry.shape, BF16),
            pltpu.VMEM(row_dosage.shape, BF16),
            pltpu.VMEM(row_ancestry.shape, BF16),
            pltpu.VMEM((8, nv, 128), F32),
            pltpu.VMEM((2, 8, nv), F32),
            pltpu.VMEM((np_, 8, nv), F32),
            pltpu.VMEM((8, nv), F32),
            pltpu.VMEM((na, nv, 128), F32),
            pltpu.VMEM((nz, 8, 128), F32),
            pltpu.VMEM((2 + 2 * na, rows, nv), BF16),
            pltpu.VMEM((2 + 2 * na, np_, nr, piece, kv), BF16),
            pltpu.VMEM((na, nr, np_, piece, kv), BF16),
            pltpu.VMEM((na, nr, piece, nz * kv), BF16),
            pltpu.VMEM((na, nr, tall, nz * kv), BF16),
            pltpu.VMEM((tall, nz * kv), BF16),
            pltpu.VMEM((chunks, nz * kv, wide), BF16),
            pltpu.VMEM((chunks, tall, wide), F32),
            pltpu.VMEM((chunks, tall, wide), F32),
            dma((4,)),
            dma((2, 1)),
            dma((2, 2, nx)),
            dma((2, nz)),
            dma((2, 2, np_, nr)),
            dma((2, na, 2, nz)),
            dma((2, na, 2, 2)),
            dma((2, na, 2, nx)),
            dma((2, na, 2, nx)),
            dma((2, 2)),
            dma((2, chunks, 2, far)),
            dma((2, chunks)),
        ],
        compiler_params=pltpu.CompilerParams(
            collective_id=0, has_side_effects=True, vmem_limit_bytes=44 * 1024 * 1024
        ),
    )(*args)
    return jnp.transpose(total / spread[:, None, :], (1, 0, 2))


def solution(mesh):
    sizes = (mesh.shape["samp"], mesh.shape["var"], mesh.shape["row"])
    placed = (
        P(None, "var", "samp"),
        P(None, None, "var", "samp"),
        P(None, "var", ("row", "samp")),
        P(None, None, "var", ("row", "samp")),
    )
    return jax.shard_map(
        functools.partial(local, sizes),
        mesh=mesh,
        in_specs=placed,
        out_specs=P(("row", "var"), None, "samp"),
        check_vma=False,
    )
```

```python
import functools

import jax
import jax.numpy as jnp
from jax import lax
from jax.experimental import pallas as pl
from jax.experimental.pallas import tpu as pltpu
from jax.sharding import PartitionSpec as P

MESH = pl.DeviceIdType.MESH
F32 = jnp.float32
BF16 = jnp.bfloat16
PARTS = 4
WHOLE = 2
STEP = 32


def device(s, z, r):
    return {"samp": s, "var": z, "row": r}


def aligned(value, size):
    return pl.multiple_of(value, size)


def kernel(
    sizes,
    cd_hbm,
    ca_hbm,
    rd_hbm,
    ra_hbm,
    o_buf,
    spread_ref,
    cd,
    ca,
    rd,
    ra,
    pst,
    part,
    stat,
    ratios,
    freq,
    spreads,
    turned,
    raw,
    centred,
    hold,
    a_buf,
    a_far,
    b_buf,
    c_send,
    c_recv,
    in_sem,
    pair_sem,
    stat_sem,
    spread_sem,
    t1_sem,
    t2_sem,
    g1_sem,
    g2_sem,
    f_sem,
    s_sem,
    b_sem,
    c_sem,
):
    ns, nz, nr = sizes
    nx, np_ = ns // 4, ns // 2
    s, z, r = lax.axis_index("samp"), lax.axis_index("var"), lax.axis_index("row")
    x, h, c = s // 4, (s // 2) % 2, s % 2
    p = s // 2
    other = 1 - r
    na = ca.shape[0]
    nv, cols = cd.shape[1:]
    kv = nv // nr
    wide = cols // PARTS
    piece = rd.shape[2] // np_
    far = nz // 2
    sibling = device(s + 1 - 2 * c, z, r)
    mate = device(s, z, other)
    across = device((x * 2 + 1 - h) * 2 + c, z, other)

    def chip(q):
        return q * 2 + c

    loads = [
        pltpu.make_async_copy(src, dst, in_sem.at[i])
        for i, (src, dst) in enumerate(((cd_hbm, cd), (ca_hbm, ca), (rd_hbm, rd), (ra_hbm, ra)))
    ]
    for load in loads:
        load.start()

    barrier = pltpu.get_barrier_semaphore()

    def greet(who):
        pl.semaphore_signal(barrier, inc=1, device_id=who, device_id_type=MESH)

    greet(sibling)
    for i in range(1, nz):
        greet(device(s, (z + i) % nz, r))
    for i in range(np_):
        for k in range(nr):
            if i or k:
                greet(device(chip((p + i) % np_), z, (r + k) % nr))

    loads[0].wait()
    loads[1].wait()

    def fold(value):
        total = value[:, :128]
        for t in range(1, cols // 128):
            total = total + value[:, t * 128:(t + 1) * 128]
        return total

    def stats(i, carry):
        rows = pl.ds(aligned(i * STEP, STEP), STEP)
        dosage = [cd[k, rows, :].astype(F32) for k in range(2)]
        for a in range(na):
            share = [ca[a, k, rows, :].astype(F32) for k in range(2)]
            pst[a, rows, :] = fold(share[0] + share[1])
            pst[4 + a, rows, :] = fold(share[0] * dosage[0] + share[1] * dosage[1])
        return carry

    lax.fori_loop(0, nv // STEP, stats, 0)
    for a in range(na):
        for k in (a, 4 + a):
            part[c, k:k + 1, :] = jnp.sum(pst[k].T, axis=0, keepdims=True)
    for k in (3, 7):
        part[c, k:k + 1, :] = jnp.ones((1, nv), F32)

    loads[2].wait()
    loads[3].wait()
    for k in range(2):
        turned[k] = rd[k].astype(F32).T.astype(BF16)
        for a in range(na):
            turned[2 + 2 * a + k] = ra[a, k].astype(F32).T.astype(BF16)

    pl.semaphore_wait(barrier, 1 + (nz - 1) + np_ * nr - 1)

    sent = []

    def push(src, dst, sems, who):
        copy = pltpu.make_async_remote_copy(
            src_ref=src, dst_ref=dst, send_sem=sems[0], recv_sem=sems[1], device_id=who, device_id_type=MESH
        )
        copy.start()
        sent.append(copy)

    def pair(ref, *at):
        return ref.at[(0, *at)], ref.at[(1, *at)]

    def arrive(dst, sems):
        pltpu.make_async_copy(dst, dst, sems[1]).wait()

    push(part.at[c], part.at[c], pair(pair_sem, 0), sibling)

    arrive(part.at[1 - c], pair(pair_sem, 0))
    stat[p] = part[0] + part[1]
    for i in range(1, nx):
        push(stat.at[p], stat.at[p], pair(stat_sem, 0, i), device(chip(((x + i) % nx) * 2 + h), z, r))
    for i in range(nx):
        push(stat.at[p], stat.at[p], pair(stat_sem, 1, i), device(chip(((x + i) % nx) * 2 + 1 - h), z, other))

    kinds = (pl.ds(0, 4), pl.ds(4, 2 * na - 2))

    def t1_piece(g, i, k):
        rows = pl.ds(aligned(((p + i) % np_) * piece, piece), piece)
        half = pl.ds(aligned((1 - (r + k) % nr) * kv, kv), kv)
        return turned.at[kinds[g], rows, half], raw.at[kinds[g], p, r]

    for g in range(2):
        pltpu.make_async_copy(*t1_piece(g, 0, 0), t1_sem.at[1, g, 0, 0]).start()
        for k in range(nr):
            for i in range(np_):
                if i or k:
                    push(*t1_piece(g, i, k), pair(t1_sem, g, i, k), device(chip((p + i) % np_), z, (r + k) % nr))

    def t1_wait(g, k):
        for i in range(np_):
            arrive(raw.at[kinds[g], (p + np_ - i) % np_, (r + nr - k) % nr], pair(t1_sem, g, i, k))

    for i in range(1, nx):
        arrive(stat.at[((x + nx - i) % nx) * 2 + h], pair(stat_sem, 0, i))
    for i in range(nx):
        arrive(stat.at[((x + nx - i) % nx) * 2 + 1 - h], pair(stat_sem, 1, i))
    total = stat[0]
    for i in range(1, np_):
        total = total + stat[i]
    ratio = total[4:8] / total[0:4]
    ratios[0:4, :] = ratio
    for a in range(na):
        freq[a] = jnp.broadcast_to(ratio[a:a + 1, :], (128, nv)).T

    def centre_rows(a, o):
        ry = r if o == 0 else other
        f = ratios[a:a + 1, pl.ds(aligned(other * kv, kv), kv)]
        f = jnp.broadcast_to(f, (piece, kv))[None]
        value = raw[2 + 2 * a, :, ry].astype(F32) * (raw[0, :, ry].astype(F32) - f)
        value = value + raw[3 + 2 * a, :, ry].astype(F32) * (raw[1, :, ry].astype(F32) - f)
        centred[a, o] = value.astype(BF16)
        hold[a, o, :, pl.ds(aligned(z * kv, kv), kv)] = centred[a, o, z]

    def hold_from(a, o, zz):
        return hold.at[a, o, :, pl.ds(aligned(zz * kv, kv), kv)]

    def t2_send(a, o):
        for i in range(1, nz):
            to = (z + i) % nz
            push(centred.at[a, o, to], hold_from(a, o, z), pair(t2_sem, a, o, i), device(s, to, r))

    def a_rows(a, o, core, first, count):
        rows = pl.ds(aligned(core * 128 + first * piece, piece), count * piece)
        if (a, o) == (na - 1, 0):
            return a_far.at[rows, :]
        return a_buf.at[a, other if o == 0 else r, rows, :]

    def t2_wait(a, o):
        for i in range(1, nz):
            arrive(hold_from(a, o, (z + nz - i) % nz), pair(t2_sem, a, o, i))

    def g1_send(a, o):
        if (a, o) == (na - 1, 0):
            a_far[pl.ds(aligned(c * 128 + p * piece, piece), piece), :] = hold[a, o]
            push(hold.at[a, o], a_rows(a, o, c, p, 1), pair(g1_sem, a, o, 1), device(chip(x * 2 + 1 - h), z, r))
            return
        rows = pl.ds(aligned(c * 128 + p * piece, piece), piece)
        dst = a_buf.at[a, r if o == 0 else other, rows, :]
        for k, who in enumerate((mate, across)):
            push(hold.at[a, o], dst, pair(g1_sem, a, o, k), who)

    def g1_wait(a, o):
        if (a, o) != (na - 1, 0):
            arrive(a_rows(a, o, c, p, 1), pair(g1_sem, a, o, 0))
        arrive(a_rows(a, o, c, x * 2 + 1 - h, 1), pair(g1_sem, a, o, 1))

    def g2_send(a, o):
        ref = a_rows(a, o, c, x * 2, 2)
        for i in range(1, nx):
            push(ref, ref, pair(g2_sem, a, o, i), device(chip(((x + i) % nx) * 2 + h), z, r))
        push(ref, ref, pair(f_sem, a, o, 0), sibling)

    def g2_wait(a, o):
        for i in range(1, nx):
            ref = a_rows(a, o, c, ((x + nx - i) % nx) * 2, 2)
            arrive(ref, pair(g2_sem, a, o, i))
            push(ref, ref, pair(f_sem, a, o, i), sibling)

    def f_wait(a, o):
        for i in range(nx):
            arrive(a_rows(a, o, 1 - c, ((x + nx - i) % nx) * 2, 2), pair(f_sem, a, o, i))

    chunks = [(a, half, False) for a in range(na) for half in range(PARTS)]
    last = [(na - 1) * PARTS + i for i in range(PARTS)]
    shared = last[:PARTS - WHOLE]
    chunks += [(na - 1, i, True) for i in range(PARTS)]

    def centre_cols(j):
        a, half, extra = chunks[j]
        first = (other if extra else r) * kv
        lanes = pl.ds(half * wide, wide)

        def body(i, carry):
            at = pl.ds(aligned(first + i * STEP, STEP), STEP)
            to = pl.ds(aligned(z * kv + i * STEP, STEP), STEP)
            f = freq[a, at, :]
            f = jnp.concatenate([f] * (wide // 128), axis=1)
            value = ca[a, 0, at, lanes].astype(F32) * (cd[0, at, lanes].astype(F32) - f)
            value = value + ca[a, 1, at, lanes].astype(F32) * (cd[1, at, lanes].astype(F32) - f)
            b_buf[j, to, :] = value.astype(BF16)
            return carry

        lax.fori_loop(0, kv // STEP, body, 0)

    ways = (1, nz - 1)

    def b_part(j, zz, way, d):
        first, count = (way * (kv // 2), kv // 2) if d == far else (0, kv)
        return b_buf.at[j, pl.ds(aligned(zz * kv + first, 64), count), :]

    def b_move(j, way, d):
        ref = b_part(j, (z + (nz - ways[way]) * (d - 1)) % nz, way, d)
        push(ref, ref, pair(b_sem, j, way, d - 1), device(s, (z + ways[way]) % nz, r))

    def launch(j):
        for way in range(2):
            b_move(j, way, 1)

    def hop(j, d):
        for way in range(2):
            zz = (z + (nz - ways[way]) * d) % nz
            arrive(b_part(j, zz, way, d), pair(b_sem, j, way, d - 1))
            if d < far:
                b_move(j, way, d + 1)
            if j in shared:
                push(b_part(j, zz, way, d), b_part(j + PARTS, zz, way, d), pair(s_sem, j - last[0], way, d - 1), mate)

    def share_wait(j):
        for d in range(1, far + 1):
            for way in range(2):
                zz = (z + (nz - ways[way]) * d) % nz
                arrive(b_part(j + PARTS, zz, way, d), pair(s_sem, j - last[0], way, d - 1))

    def hand_over(j):
        a = chunks[j][0]
        c_send[j] = jnp.dot(a_buf[a, other], b_buf[j], preferred_element_type=F32)
        push(c_send.at[j], c_recv.at[j], pair(c_sem, j), mate)

    def out_lanes(j):
        return pl.ds(chunks[j][1] * wide, wide)

    def keep(j):
        a = chunks[j][0]
        o_buf[a, :, out_lanes(j)] = jnp.dot(a_buf[a, r], b_buf[j], preferred_element_type=F32)

    def both(j, extra):
        a = chunks[j][0]
        if j in shared:
            share_wait(j)
        value = jnp.dot(a_buf[a, r], b_buf[j], preferred_element_type=F32)
        o_buf[a, :, out_lanes(j)] = value + jnp.dot(a_far[...], b_buf[extra], preferred_element_type=F32)

    def finish(j):
        a = chunks[j][0]
        arrive(c_recv.at[j], pair(c_sem, j))
        o_buf[a, :, out_lanes(j)] += c_recv[j]

    def share_spread():
        spreads[z, 0:4, :] = jnp.broadcast_to(jnp.sum(ratio * (1.0 - ratio), axis=1, keepdims=True), (4, 128))
        spreads[z, 4:8, :] = jnp.zeros((4, 128), F32)
        for i in range(1, nz):
            push(spreads.at[z], spreads.at[z], pair(spread_sem, i), device(s, (z + i) % nz, r))

    centre_cols(0)
    launch(0)
    centre_cols(1)
    launch(1)
    centre_cols(8)
    launch(8)
    share_spread()
    centre_cols(12)
    centre_cols(13)
    centre_cols(9)
    launch(9)
    t1_wait(0, 0)
    centre_rows(0, 0)
    t2_send(0, 0)
    hop(0, 1)
    t1_wait(1, 0)
    centre_rows(1, 0)
    t2_send(1, 0)
    centre_rows(2, 0)
    t2_send(2, 0)
    hop(1, 1)
    hop(8, 1)
    t1_wait(0, 1)
    centre_rows(0, 1)
    t2_send(0, 1)
    hop(9, 1)
    t1_wait(1, 1)
    centre_rows(2, 1)
    t2_send(2, 1)
    centre_rows(1, 1)
    t2_send(1, 1)
    hop(0, 2)
    hop(1, 2)
    t2_wait(0, 0)
    g1_send(0, 0)
    hop(8, 2)
    t2_wait(1, 0)
    g1_send(1, 0)
    hop(9, 2)
    t2_wait(2, 0)
    g1_send(2, 0)
    centre_cols(2)
    launch(2)
    centre_cols(3)
    launch(3)
    g1_wait(0, 0)
    g2_send(0, 0)
    hop(0, 3)
    hop(1, 3)
    t2_wait(0, 1)
    g1_send(0, 1)
    centre_cols(4)
    launch(4)
    hop(8, 3)
    hop(9, 3)
    g1_wait(1, 0)
    g2_send(1, 0)
    hop(2, 1)
    t2_wait(1, 1)
    g1_send(1, 1)
    hop(3, 1)
    hop(0, 4)
    hop(1, 4)
    t2_wait(2, 1)
    g1_send(2, 1)
    centre_cols(5)
    launch(5)
    g1_wait(0, 1)
    g2_send(0, 1)
    hop(8, 4)
    hop(9, 4)
    hop(2, 2)
    hop(4, 1)
    g2_wait(0, 0)
    hop(3, 2)
    g1_wait(2, 0)
    g2_send(2, 0)
    centre_cols(6)
    launch(6)
    hop(5, 1)
    g1_wait(1, 1)
    g2_send(1, 1)
    f_wait(0, 0)
    hand_over(0)
    hand_over(1)
    hop(2, 3)
    g2_wait(1, 0)
    centre_cols(7)
    launch(7)
    centre_cols(10)
    launch(10)
    hop(4, 2)
    hop(3, 3)
    g1_wait(2, 1)
    g2_send(2, 1)
    f_wait(1, 0)
    hop(6, 1)
    hop(5, 2)
    g2_wait(0, 1)
    hop(2, 4)
    hand_over(2)
    hop(7, 1)
    hop(10, 1)
    f_wait(0, 1)
    keep(0)
    hop(4, 3)
    keep(1)
    hop(3, 4)
    hand_over(3)
    centre_cols(14)
    launch(14)
    g2_wait(2, 0)
    centre_cols(11)
    launch(11)
    centre_cols(15)
    launch(15)
    hop(5, 3)
    hop(6, 2)
    hop(7, 2)
    hop(10, 2)
    hop(4, 4)
    hand_over(4)
    g2_wait(1, 1)
    hop(14, 1)
    f_wait(2, 0)
    keep(2)
    hop(11, 1)
    keep(3)
    hop(15, 1)
    f_wait(1, 1)
    hop(5, 4)
    hand_over(5)
    g2_wait(2, 1)
    hop(6, 3)
    keep(4)
    hop(7, 3)
    keep(5)
    finish(0)
    hop(10, 3)
    f_wait(2, 1)
    both(8, 12)
    hop(14, 2)
    both(9, 13)
    hop(11, 2)
    hop(15, 2)
    hop(6, 4)
    hand_over(6)
    hop(7, 4)
    hand_over(7)
    hop(10, 4)
    keep(6)
    hop(14, 3)
    keep(7)
    finish(1)
    finish(2)
    hop(11, 3)
    finish(3)
    finish(4)
    finish(5)
    hop(15, 3)
    hop(14, 4)
    both(10, 14)
    hop(11, 4)
    finish(6)
    hop(15, 4)
    both(11, 15)
    finish(7)

    for i in range(1, nz):
        arrive(spreads.at[(z + nz - i) % nz], pair(spread_sem, i))
    spread = spreads[0]
    for i in range(1, nz):
        spread = spread + spreads[i]
    for a in range(na):
        spread_ref[a:a + 1, :] = jnp.concatenate([spread[a:a + 1, :]] * (cols // 128), axis=1)
    for copy in sent:
        copy.wait_send()


def local(sizes, col_dosage, col_ancestry, row_dosage, row_ancestry):
    ns, nz, nr = sizes
    nx, np_ = ns // 4, ns // 2
    na = col_ancestry.shape[0]
    nv, cols = col_dosage.shape[1:]
    rows = row_dosage.shape[2]
    kv = nv // nr
    tall = 2 * rows
    wide = cols // PARTS
    piece = rows // np_
    chunks = (na + 1) * PARTS
    far = nz // 2
    dma = pltpu.SemaphoreType.DMA
    args = (col_dosage, col_ancestry, row_dosage, row_ancestry)
    args = [pltpu.with_memory_space_constraint(v, pltpu.HBM) for v in args]
    total, spread = pl.pallas_call(
        functools.partial(kernel, sizes),
        out_shape=(
            pltpu.VMEM((na, tall, cols), F32),
            jax.ShapeDtypeStruct((na, cols), F32),
        ),
        in_specs=[pl.BlockSpec(memory_space=pltpu.HBM)] * 4,
        out_specs=(pl.BlockSpec(memory_space=pltpu.VMEM), pl.BlockSpec(memory_space=pltpu.VMEM)),
        scratch_shapes=[
            pltpu.VMEM(col_dosage.shape, BF16),
            pltpu.VMEM(col_ancestry.shape, BF16),
            pltpu.VMEM(row_dosage.shape, BF16),
            pltpu.VMEM(row_ancestry.shape, BF16),
            pltpu.VMEM((8, nv, 128), F32),
            pltpu.VMEM((2, 8, nv), F32),
            pltpu.VMEM((np_, 8, nv), F32),
            pltpu.VMEM((8, nv), F32),
            pltpu.VMEM((na, nv, 128), F32),
            pltpu.VMEM((nz, 8, 128), F32),
            pltpu.VMEM((2 + 2 * na, rows, nv), BF16),
            pltpu.VMEM((2 + 2 * na, np_, nr, piece, kv), BF16),
            pltpu.VMEM((na, nr, np_, piece, kv), BF16),
            pltpu.VMEM((na, nr, piece, nz * kv), BF16),
            pltpu.VMEM((na, nr, tall, nz * kv), BF16),
            pltpu.VMEM((tall, nz * kv), BF16),
            pltpu.VMEM((chunks, nz * kv, wide), BF16),
            pltpu.VMEM(((na - 1) * PARTS, tall, wide), F32),
            pltpu.VMEM(((na - 1) * PARTS, tall, wide), F32),
            dma((4,)),
            dma((2, 1)),
            dma((2, 2, nx)),
            dma((2, nz)),
            dma((2, 2, np_, nr)),
            dma((2, na, 2, nz)),
            dma((2, na, 2, 2)),
            dma((2, na, 2, nx)),
            dma((2, na, 2, nx)),
            dma((2, PARTS, 2, far)),
            dma((2, chunks, 2, far)),
            dma((2, (na - 1) * PARTS)),
        ],
        compiler_params=pltpu.CompilerParams(
            collective_id=0, has_side_effects=True, vmem_limit_bytes=44 * 1024 * 1024
        ),
    )(*args)
    return jnp.transpose(total / spread[:, None, :], (1, 0, 2))


def solution(mesh):
    sizes = (mesh.shape["samp"], mesh.shape["var"], mesh.shape["row"])
    placed = (
        P(None, "var", "samp"),
        P(None, None, "var", "samp"),
        P(None, "var", ("row", "samp")),
        P(None, None, "var", ("row", "samp")),
    )
    return jax.shard_map(
        functools.partial(local, sizes),
        mesh=mesh,
        in_specs=placed,
        out_specs=P(("row", "var"), None, "samp"),
        check_vma=False,
    )
```

```python
import functools

import jax
import jax.numpy as jnp
from jax import lax
from jax.experimental import pallas as pl
from jax.experimental.pallas import tpu as pltpu
from jax.sharding import PartitionSpec as P

MESH = pl.DeviceIdType.MESH
F32 = jnp.float32
BF16 = jnp.bfloat16
PARTS = 4
WHOLE = 2
STEP = 32


def device(s, z, r):
    return {"samp": s, "var": z, "row": r}


def aligned(value, size):
    return pl.multiple_of(value, size)


def kernel(
    sizes,
    cd_hbm,
    ca_hbm,
    rd_hbm,
    ra_hbm,
    o_buf,
    spread_ref,
    cd,
    ca,
    rd,
    ra,
    pst,
    part,
    stat,
    ratios,
    freq,
    spreads,
    turned,
    raw,
    centred,
    hold,
    a_buf,
    a_far,
    b_buf,
    c_send,
    c_recv,
    in_sem,
    pair_sem,
    stat_sem,
    spread_sem,
    t1_sem,
    t2_sem,
    g1_sem,
    g2_sem,
    f_sem,
    s_sem,
    b_sem,
    c_sem,
):
    ns, nz, nr = sizes
    nx, np_ = ns // 4, ns // 2
    s, z, r = lax.axis_index("samp"), lax.axis_index("var"), lax.axis_index("row")
    x, h, c = s // 4, (s // 2) % 2, s % 2
    p = s // 2
    other = 1 - r
    na = ca.shape[0]
    nv, cols = cd.shape[1:]
    kv = nv // nr
    wide = cols // PARTS
    piece = rd.shape[2] // np_
    far = nz // 2
    sibling = device(s + 1 - 2 * c, z, r)
    mate = device(s, z, other)
    across = device((x * 2 + 1 - h) * 2 + c, z, other)

    def chip(q):
        return q * 2 + c

    loads = [
        pltpu.make_async_copy(src, dst, in_sem.at[i])
        for i, (src, dst) in enumerate(((cd_hbm, cd), (ca_hbm, ca), (rd_hbm, rd), (ra_hbm, ra)))
    ]
    for load in loads:
        load.start()

    barrier = pltpu.get_barrier_semaphore()

    def greet(who):
        pl.semaphore_signal(barrier, inc=1, device_id=who, device_id_type=MESH)

    greet(sibling)
    for i in range(1, nz):
        greet(device(s, (z + i) % nz, r))
    for i in range(np_):
        for k in range(nr):
            if i or k:
                greet(device(chip((p + i) % np_), z, (r + k) % nr))

    loads[0].wait()
    loads[1].wait()

    def fold(value):
        total = value[:, :128]
        for t in range(1, cols // 128):
            total = total + value[:, t * 128:(t + 1) * 128]
        return total

    def stats(i, carry):
        rows = pl.ds(aligned(i * STEP, STEP), STEP)
        dosage = [cd[k, rows, :].astype(F32) for k in range(2)]
        for a in range(na):
            share = [ca[a, k, rows, :].astype(F32) for k in range(2)]
            pst[a, rows, :] = fold(share[0] + share[1])
            pst[4 + a, rows, :] = fold(share[0] * dosage[0] + share[1] * dosage[1])
        return carry

    lax.fori_loop(0, nv // STEP, stats, 0)
    for a in range(na):
        for k in (a, 4 + a):
            part[c, k:k + 1, :] = jnp.sum(pst[k].T, axis=0, keepdims=True)
    for k in (3, 7):
        part[c, k:k + 1, :] = jnp.ones((1, nv), F32)

    loads[2].wait()
    loads[3].wait()
    for k in range(2):
        turned[k] = rd[k].astype(F32).T.astype(BF16)
        for a in range(na):
            turned[2 + 2 * a + k] = ra[a, k].astype(F32).T.astype(BF16)

    pl.semaphore_wait(barrier, 1 + (nz - 1) + np_ * nr - 1)

    sent = []

    def push(src, dst, sems, who):
        copy = pltpu.make_async_remote_copy(
            src_ref=src, dst_ref=dst, send_sem=sems[0], recv_sem=sems[1], device_id=who, device_id_type=MESH
        )
        copy.start()
        sent.append(copy)

    def pair(ref, *at):
        return ref.at[(0, *at)], ref.at[(1, *at)]

    def arrive(dst, sems):
        pltpu.make_async_copy(dst, dst, sems[1]).wait()

    push(part.at[c], part.at[c], pair(pair_sem, 0), sibling)

    arrive(part.at[1 - c], pair(pair_sem, 0))
    stat[p] = part[0] + part[1]
    for i in sorted(range(nx), key=lambda i: -min(i, nx - i)):
        push(stat.at[p], stat.at[p], pair(stat_sem, 1, i), device(chip(((x + i) % nx) * 2 + 1 - h), z, other))
        if i:
            push(stat.at[p], stat.at[p], pair(stat_sem, 0, i), device(chip(((x + i) % nx) * 2 + h), z, r))

    kinds = (pl.ds(0, 4), pl.ds(4, 2 * na - 2))

    def t1_piece(g, i, k):
        rows = pl.ds(aligned(((p + i) % np_) * piece, piece), piece)
        half = pl.ds(aligned((1 - (r + k) % nr) * kv, kv), kv)
        return turned.at[kinds[g], rows, half], raw.at[kinds[g], p, r]

    for g in range(2):
        pltpu.make_async_copy(*t1_piece(g, 0, 0), t1_sem.at[1, g, 0, 0]).start()
        for k in range(nr):
            for i in range(np_):
                if i or k:
                    push(*t1_piece(g, i, k), pair(t1_sem, g, i, k), device(chip((p + i) % np_), z, (r + k) % nr))

    def t1_wait(g, k):
        for i in range(np_):
            arrive(raw.at[kinds[g], (p + np_ - i) % np_, (r + nr - k) % nr], pair(t1_sem, g, i, k))

    for i in range(1, nx):
        arrive(stat.at[((x + nx - i) % nx) * 2 + h], pair(stat_sem, 0, i))
    for i in range(nx):
        arrive(stat.at[((x + nx - i) % nx) * 2 + 1 - h], pair(stat_sem, 1, i))
    total = stat[0]
    for i in range(1, np_):
        total = total + stat[i]
    ratio = total[4:8] / total[0:4]
    ratios[0:4, :] = ratio
    for a in range(na):
        freq[a] = jnp.broadcast_to(ratio[a:a + 1, :], (128, nv)).T

    def centre_rows(a, o):
        ry = r if o == 0 else other
        f = ratios[a:a + 1, pl.ds(aligned(other * kv, kv), kv)]
        f = jnp.broadcast_to(f, (piece, kv))[None]
        value = raw[2 + 2 * a, :, ry].astype(F32) * (raw[0, :, ry].astype(F32) - f)
        value = value + raw[3 + 2 * a, :, ry].astype(F32) * (raw[1, :, ry].astype(F32) - f)
        centred[a, o] = value.astype(BF16)
        hold[a, o, :, pl.ds(aligned(z * kv, kv), kv)] = centred[a, o, z]

    def hold_from(a, o, zz):
        return hold.at[a, o, :, pl.ds(aligned(zz * kv, kv), kv)]

    def t2_send(a, o):
        for i in sorted(range(1, nz), key=lambda i: -min(i, nz - i)):
            to = (z + i) % nz
            push(centred.at[a, o, to], hold_from(a, o, z), pair(t2_sem, a, o, i), device(s, to, r))

    def a_rows(a, o, core, first, count):
        rows = pl.ds(aligned(core * 128 + first * piece, piece), count * piece)
        if (a, o) == (na - 1, 0):
            return a_far.at[rows, :]
        return a_buf.at[a, other if o == 0 else r, rows, :]

    def t2_wait(a, o):
        for i in range(1, nz):
            arrive(hold_from(a, o, (z + nz - i) % nz), pair(t2_sem, a, o, i))

    def g1_send(a, o):
        if (a, o) == (na - 1, 0):
            a_far[pl.ds(aligned(c * 128 + p * piece, piece), piece), :] = hold[a, o]
            push(hold.at[a, o], a_rows(a, o, c, p, 1), pair(g1_sem, a, o, 1), device(chip(x * 2 + 1 - h), z, r))
            return
        rows = pl.ds(aligned(c * 128 + p * piece, piece), piece)
        dst = a_buf.at[a, r if o == 0 else other, rows, :]
        for k, who in enumerate((mate, across)):
            push(hold.at[a, o], dst, pair(g1_sem, a, o, k), who)

    def g1_wait(a, o):
        if (a, o) != (na - 1, 0):
            arrive(a_rows(a, o, c, p, 1), pair(g1_sem, a, o, 0))
        arrive(a_rows(a, o, c, x * 2 + 1 - h, 1), pair(g1_sem, a, o, 1))

    def g2_send(a, o):
        ref = a_rows(a, o, c, x * 2, 2)
        for i in sorted(range(1, nx), key=lambda i: -min(i, nx - i)):
            push(ref, ref, pair(g2_sem, a, o, i), device(chip(((x + i) % nx) * 2 + h), z, r))
        push(ref, ref, pair(f_sem, a, o, 0), sibling)

    def g2_wait(a, o):
        for i in range(1, nx):
            ref = a_rows(a, o, c, ((x + nx - i) % nx) * 2, 2)
            arrive(ref, pair(g2_sem, a, o, i))
            push(ref, ref, pair(f_sem, a, o, i), sibling)

    def f_wait(a, o):
        for i in range(nx):
            arrive(a_rows(a, o, 1 - c, ((x + nx - i) % nx) * 2, 2), pair(f_sem, a, o, i))

    chunks = [(a, half, False) for a in range(na) for half in range(PARTS)]
    last = [(na - 1) * PARTS + i for i in range(PARTS)]
    shared = last[:PARTS - WHOLE]
    chunks += [(na - 1, i, True) for i in range(PARTS)]

    def centre_cols(j):
        a, half, extra = chunks[j]
        first = (other if extra else r) * kv
        lanes = pl.ds(half * wide, wide)

        def body(i, carry):
            at = pl.ds(aligned(first + i * STEP, STEP), STEP)
            to = pl.ds(aligned(z * kv + i * STEP, STEP), STEP)
            f = freq[a, at, :]
            f = jnp.concatenate([f] * (wide // 128), axis=1)
            value = ca[a, 0, at, lanes].astype(F32) * (cd[0, at, lanes].astype(F32) - f)
            value = value + ca[a, 1, at, lanes].astype(F32) * (cd[1, at, lanes].astype(F32) - f)
            b_buf[j, to, :] = value.astype(BF16)
            return carry

        lax.fori_loop(0, kv // STEP, body, 0)

    ways = (1, nz - 1)

    def b_part(j, zz, way, d):
        first, count = (way * (kv // 2), kv // 2) if d == far else (0, kv)
        return b_buf.at[j, pl.ds(aligned(zz * kv + first, 64), count), :]

    def b_move(j, way, d):
        ref = b_part(j, (z + (nz - ways[way]) * (d - 1)) % nz, way, d)
        push(ref, ref, pair(b_sem, j, way, d - 1), device(s, (z + ways[way]) % nz, r))

    def launch(j):
        for way in range(2):
            b_move(j, way, 1)

    def hop(j, d):
        for way in range(2):
            zz = (z + (nz - ways[way]) * d) % nz
            arrive(b_part(j, zz, way, d), pair(b_sem, j, way, d - 1))
            if d < far:
                b_move(j, way, d + 1)
            if j in shared:
                push(b_part(j, zz, way, d), b_part(j + PARTS, zz, way, d), pair(s_sem, j - last[0], way, d - 1), mate)

    def share_wait(j):
        for d in range(1, far + 1):
            for way in range(2):
                zz = (z + (nz - ways[way]) * d) % nz
                arrive(b_part(j + PARTS, zz, way, d), pair(s_sem, j - last[0], way, d - 1))

    def hand_over(j):
        a = chunks[j][0]
        c_send[j] = jnp.dot(a_buf[a, other], b_buf[j], preferred_element_type=F32)
        push(c_send.at[j], c_recv.at[j], pair(c_sem, j), mate)

    def out_lanes(j):
        return pl.ds(chunks[j][1] * wide, wide)

    def keep(j):
        a = chunks[j][0]
        o_buf[a, :, out_lanes(j)] = jnp.dot(a_buf[a, r], b_buf[j], preferred_element_type=F32)

    def both(j, extra):
        a = chunks[j][0]
        if j in shared:
            share_wait(j)
        value = jnp.dot(a_buf[a, r], b_buf[j], preferred_element_type=F32)
        o_buf[a, :, out_lanes(j)] = value + jnp.dot(a_far[...], b_buf[extra], preferred_element_type=F32)

    def finish(j):
        a = chunks[j][0]
        arrive(c_recv.at[j], pair(c_sem, j))
        o_buf[a, :, out_lanes(j)] += c_recv[j]

    def share_spread():
        spreads[z, 0:4, :] = jnp.broadcast_to(jnp.sum(ratio * (1.0 - ratio), axis=1, keepdims=True), (4, 128))
        spreads[z, 4:8, :] = jnp.zeros((4, 128), F32)
        for i in range(1, nz):
            push(spreads.at[z], spreads.at[z], pair(spread_sem, i), device(s, (z + i) % nz, r))

    centre_cols(0)
    launch(0)
    centre_cols(1)
    launch(1)
    centre_cols(8)
    launch(8)
    share_spread()
    centre_cols(12)
    centre_cols(13)
    centre_cols(9)
    launch(9)
    t1_wait(0, 0)
    centre_rows(0, 0)
    t2_send(0, 0)
    hop(0, 1)
    t1_wait(1, 0)
    centre_rows(1, 0)
    t2_send(1, 0)
    centre_rows(2, 0)
    t2_send(2, 0)
    hop(1, 1)
    hop(8, 1)
    t1_wait(0, 1)
    centre_rows(0, 1)
    t2_send(0, 1)
    hop(9, 1)
    t1_wait(1, 1)
    centre_rows(2, 1)
    t2_send(2, 1)
    centre_rows(1, 1)
    t2_send(1, 1)
    hop(0, 2)
    hop(1, 2)
    t2_wait(0, 0)
    g1_send(0, 0)
    hop(8, 2)
    t2_wait(1, 0)
    g1_send(1, 0)
    hop(9, 2)
    t2_wait(2, 0)
    g1_send(2, 0)
    centre_cols(2)
    launch(2)
    centre_cols(3)
    launch(3)
    g1_wait(0, 0)
    g2_send(0, 0)
    hop(0, 3)
    hop(1, 3)
    t2_wait(0, 1)
    g1_send(0, 1)
    centre_cols(4)
    launch(4)
    hop(8, 3)
    hop(9, 3)
    g1_wait(1, 0)
    g2_send(1, 0)
    hop(2, 1)
    t2_wait(1, 1)
    g1_send(1, 1)
    hop(3, 1)
    hop(0, 4)
    hop(1, 4)
    t2_wait(2, 1)
    g1_send(2, 1)
    centre_cols(5)
    launch(5)
    g1_wait(0, 1)
    g2_send(0, 1)
    hop(8, 4)
    hop(9, 4)
    hop(2, 2)
    hop(4, 1)
    g2_wait(0, 0)
    hop(3, 2)
    g1_wait(2, 0)
    g2_send(2, 0)
    centre_cols(6)
    launch(6)
    hop(5, 1)
    g1_wait(1, 1)
    g2_send(1, 1)
    f_wait(0, 0)
    hand_over(0)
    hand_over(1)
    hop(2, 3)
    g2_wait(1, 0)
    centre_cols(7)
    launch(7)
    centre_cols(10)
    launch(10)
    hop(4, 2)
    hop(3, 3)
    g1_wait(2, 1)
    g2_send(2, 1)
    f_wait(1, 0)
    hop(6, 1)
    hop(5, 2)
    g2_wait(0, 1)
    hop(2, 4)
    hand_over(2)
    hop(7, 1)
    hop(10, 1)
    f_wait(0, 1)
    keep(0)
    hop(4, 3)
    keep(1)
    hop(3, 4)
    hand_over(3)
    centre_cols(14)
    launch(14)
    g2_wait(2, 0)
    centre_cols(11)
    launch(11)
    centre_cols(15)
    launch(15)
    hop(5, 3)
    hop(6, 2)
    hop(7, 2)
    hop(10, 2)
    hop(4, 4)
    hand_over(4)
    g2_wait(1, 1)
    hop(14, 1)
    f_wait(2, 0)
    keep(2)
    hop(11, 1)
    keep(3)
    hop(15, 1)
    f_wait(1, 1)
    hop(5, 4)
    hand_over(5)
    g2_wait(2, 1)
    hop(6, 3)
    keep(4)
    hop(7, 3)
    keep(5)
    finish(0)
    hop(10, 3)
    f_wait(2, 1)
    both(8, 12)
    hop(14, 2)
    both(9, 13)
    hop(11, 2)
    hop(15, 2)
    hop(6, 4)
    hand_over(6)
    hop(7, 4)
    hand_over(7)
    hop(10, 4)
    keep(6)
    hop(14, 3)
    keep(7)
    finish(1)
    finish(2)
    hop(11, 3)
    finish(3)
    finish(4)
    finish(5)
    hop(15, 3)
    hop(14, 4)
    both(10, 14)
    hop(11, 4)
    finish(6)
    hop(15, 4)
    both(11, 15)
    finish(7)

    for i in range(1, nz):
        arrive(spreads.at[(z + nz - i) % nz], pair(spread_sem, i))
    spread = spreads[0]
    for i in range(1, nz):
        spread = spread + spreads[i]
    for a in range(na):
        spread_ref[a:a + 1, :] = jnp.concatenate([spread[a:a + 1, :]] * (cols // 128), axis=1)
    for copy in sent:
        copy.wait_send()


def local(sizes, col_dosage, col_ancestry, row_dosage, row_ancestry):
    ns, nz, nr = sizes
    nx, np_ = ns // 4, ns // 2
    na = col_ancestry.shape[0]
    nv, cols = col_dosage.shape[1:]
    rows = row_dosage.shape[2]
    kv = nv // nr
    tall = 2 * rows
    wide = cols // PARTS
    piece = rows // np_
    chunks = (na + 1) * PARTS
    far = nz // 2
    dma = pltpu.SemaphoreType.DMA
    args = (col_dosage, col_ancestry, row_dosage, row_ancestry)
    args = [pltpu.with_memory_space_constraint(v, pltpu.HBM) for v in args]
    total, spread = pl.pallas_call(
        functools.partial(kernel, sizes),
        out_shape=(
            pltpu.VMEM((na, tall, cols), F32),
            jax.ShapeDtypeStruct((na, cols), F32),
        ),
        in_specs=[pl.BlockSpec(memory_space=pltpu.HBM)] * 4,
        out_specs=(pl.BlockSpec(memory_space=pltpu.VMEM), pl.BlockSpec(memory_space=pltpu.VMEM)),
        scratch_shapes=[
            pltpu.VMEM(col_dosage.shape, BF16),
            pltpu.VMEM(col_ancestry.shape, BF16),
            pltpu.VMEM(row_dosage.shape, BF16),
            pltpu.VMEM(row_ancestry.shape, BF16),
            pltpu.VMEM((8, nv, 128), F32),
            pltpu.VMEM((2, 8, nv), F32),
            pltpu.VMEM((np_, 8, nv), F32),
            pltpu.VMEM((8, nv), F32),
            pltpu.VMEM((na, nv, 128), F32),
            pltpu.VMEM((nz, 8, 128), F32),
            pltpu.VMEM((2 + 2 * na, rows, nv), BF16),
            pltpu.VMEM((2 + 2 * na, np_, nr, piece, kv), BF16),
            pltpu.VMEM((na, nr, np_, piece, kv), BF16),
            pltpu.VMEM((na, nr, piece, nz * kv), BF16),
            pltpu.VMEM((na, nr, tall, nz * kv), BF16),
            pltpu.VMEM((tall, nz * kv), BF16),
            pltpu.VMEM((chunks, nz * kv, wide), BF16),
            pltpu.VMEM(((na - 1) * PARTS, tall, wide), F32),
            pltpu.VMEM(((na - 1) * PARTS, tall, wide), F32),
            dma((4,)),
            dma((2, 1)),
            dma((2, 2, nx)),
            dma((2, nz)),
            dma((2, 2, np_, nr)),
            dma((2, na, 2, nz)),
            dma((2, na, 2, 2)),
            dma((2, na, 2, nx)),
            dma((2, na, 2, nx)),
            dma((2, PARTS, 2, far)),
            dma((2, chunks, 2, far)),
            dma((2, (na - 1) * PARTS)),
        ],
        compiler_params=pltpu.CompilerParams(
            collective_id=0, has_side_effects=True, vmem_limit_bytes=44 * 1024 * 1024
        ),
    )(*args)
    return jnp.transpose(total / spread[:, None, :], (1, 0, 2))


def solution(mesh):
    sizes = (mesh.shape["samp"], mesh.shape["var"], mesh.shape["row"])
    placed = (
        P(None, "var", "samp"),
        P(None, None, "var", "samp"),
        P(None, "var", ("row", "samp")),
        P(None, None, "var", ("row", "samp")),
    )
    return jax.shard_map(
        functools.partial(local, sizes),
        mesh=mesh,
        in_specs=placed,
        out_specs=P(("row", "var"), None, "samp"),
        check_vma=False,
    )
```
